32 devices in a mesh: site: 8 (over z, x), expert: 4 (over y, core).
Axes of the slice: x: 2, y: 2, z: 4, core: 2. Of those that a mesh axis runs over, the one named last changes fastest.
Arguments:
- out_grads: bfloat16 [2, 8, 512, 1024], P(None, 'site', 'expert'), may hold values from -6 to 6
- routes: int32 [2, 8, 512, 1], P(None, 'site', 'expert'), may hold values from 0 to 3; in each aligned block of 128 rows (0 to 127, 128 to 255, ..., all dimensions but the last counted through in order) at most 64 rows name the same one
- hiddens: bfloat16 [2, 8, 4, 256, 512], P(None, 'site', 'expert'), may hold values from -6 to 6
- weights: bfloat16 [8, 4, 512, 1024], P('site', 'expert'), may hold values from -6 to 6
- tracker_offset: bfloat16 [8, 4, 512, 1024], P('site', 'expert'), may hold values from -20 to 20
- partner_bits: int32 [8, 2], P('site'), may hold values from 0 to 1, as said below
Outputs:
- new_weights: bfloat16 [8, 4, 512, 1024], P('site', 'expert')
The draws below stay inside these ranges and needn't reach their ends.
Inputs may be any that keep to these rules, and one draw needn't show every extreme that they name: `routes`: among the 128 tokens of one device in a step no expert is named more than 64 times, a bound that some block reaches. `partner_bits`: site 0 and site 8 - 1 each take the partner ahead in exactly one of the two rounds.
All inputs are finite; a program needn't handle non-finite values.
Results may differ from the reference program's by a relative error of at most 0.0095.
Values may be sent and summed in bfloat16 or wider, within the bound.
No kernel may reach another device: no remote copies, remote signals or barrier semaphores. Data moves between devices by JAX's collectives and lax.ppermute only.
A program may use at most 64 MiB of HBM per device.

```python
import math
import jax
import jax.numpy as jnp
import numpy as np
from jax import lax

D = 1024
FF_E = 512
EXP_ROWS = 256
NS_ITERS = 2
STEPS = 2
SITES = 8
EXPERTS = 4
SLOTS = 64
TOK_DEV = 128
TOKENS = 512


def draw_tracker_offset(key, part):
    key_rows = jax.random.fold_in(key, 11)
    key_cols = jax.random.fold_in(key, 23)
    key_body = jax.random.fold_in(key, 37)
    shape = (SITES, EXPERTS, FF_E, D)
    row_scale = jnp.exp(jax.random.uniform(key_rows, (SITES, EXPERTS, FF_E, 1), jnp.float32) * math.log(10.0))
    col_scale = jnp.exp(jax.random.uniform(key_cols, (SITES, EXPERTS, 1, D), jnp.float32) * math.log(10.0))
    entries = jnp.clip(jax.random.normal(key_body, shape, jnp.float32), -4.0, 4.0) * 0.05
    return (entries * row_scale * col_scale).astype(jnp.bfloat16)


def draw_partner_bits(key, part):
    key_bits = jax.random.fold_in(key, 53)
    bits = jax.random.randint(key_bits, (SITES, 2), 0, 2, jnp.int32)
    rows = jnp.arange(SITES, dtype=jnp.int32)
    at_end = (rows == 0) | (rows == SITES - 1)
    second = jnp.where(at_end, 1 - bits[:, 0], bits[:, 1])
    return jnp.stack([bits[:, 0], second], axis=1)


def levels(own_key, dims, cuts, least, high):
    level = 1.0
    for dim, parts in cuts:
        draws = jax.random.uniform(jax.random.fold_in(jax.random.fold_in(own_key, 6), dim), (parts,), jnp.float32, least / len(cuts), high / len(cuts))
        level = level * jnp.repeat(jnp.exp(draws), dims[dim] // parts).reshape((-1,) + (1,) * (len(dims) - 1 - dim))
    return level


def shared_out(key, own, number, rows, number_of, top, bound, slope):
    order = jax.random.permutation(key, number_of)
    crowded, common = portions_of(number_of, rows * top, bound, slope, True), portions_of(number_of, rows * top, bound, slope, False)
    places = jnp.arange(number_of)

    def named(tallies, turn):
        used = int((tallies > 0).sum())
        fixed = max(1, used // 4)
        passed = fixed + (places - fixed + turn * (used - fixed)) % max(1, number_of - fixed)
        return jnp.zeros((number_of,), jnp.int32).at[order[jnp.where(places < fixed, places, passed)]].set(jnp.asarray(tallies, jnp.int32))

    tallies = jnp.where(number % 4 == 0, named(crowded, number // 4), named(common, number - number // 4 - 1))
    mixed = jax.random.permutation(jax.random.fold_in(own, 3), number_of)
    donor, receiver = mixed[0:number_of // 2 * 2:2], mixed[1:number_of // 2 * 2:2]
    margin = jnp.minimum(tallies[donor] - 1, bound - tallies[receiver]) // 2
    margin = jnp.where((donor == order[0]) | (receiver == order[0]) | (tallies[receiver] == 0), 0, jnp.maximum(margin, 0))
    passed = jax.random.randint(jax.random.fold_in(own, 4), (number_of // 2,), 0, 1 << 20) % (margin + 1)
    tallies = tallies.at[donor].add(-passed).at[receiver].add(passed)
    labels = jnp.searchsorted(jnp.cumsum(tallies), jnp.arange(rows * top), side="right").astype(jnp.int32)
    table = labels.reshape(top, rows).T
    table = table[jax.random.permutation(jax.random.fold_in(own, 1), rows)]
    turn = jax.random.randint(jax.random.fold_in(own, 2), (rows, 1), 0, top)
    return jnp.take_along_axis(table, (jnp.arange(top)[None, :] + turn) % top, axis=1)


def portions_of(amount, total, reach, slope, full):
    weights = [(1 << 20) // math.isqrt(grade ** slope) + 1 for grade in range(1, amount + 1)]
    largest = reach if full else min(reach, max(-(-total // amount), total * weights[0] // sum(weights)))
    least = 1 if total - largest >= amount - 1 else 0
    given, spare = [largest] + [least] * (amount - 1), total - largest - least * (amount - 1)
    while spare > 0:
        movable = [i for i in range(1, amount) if given[i] < largest] or [i for i in range(1, amount) if given[i] < reach]
        whole, remaining = sum([weights[i] for i in movable]), spare
        for i in movable:
            more = min(reach - given[i], max(1, remaining * weights[i] // whole), spare)
            given[i] = given[i] + more
            spare = spare - more
    return np.array(given)


def noise(own_key, shape, scale, most, split=(), kind=jnp.bfloat16):
    level = levels(own_key, shape, split, -0.22, 0.18) if split else 1.0
    values = jax.random.normal(own_key, shape, jnp.float32) * scale * level
    return jnp.minimum(jnp.maximum(values, -most), most).astype(kind)


def setup_inputs(seed: int = 0) -> dict:
    arg_keys = jax.random.split(jax.random.key(seed), 7)
    out_grads = noise(arg_keys[0], (STEPS, SITES, TOKENS, D), 1.0, 6.0, ((1, 8), (2, 4)))
    routes_keys = jax.random.split(jax.random.fold_in(arg_keys[1], 1), STEPS * SITES * TOKENS // TOK_DEV)
    routes_turns = jax.random.permutation(jax.random.fold_in(arg_keys[1], 3), STEPS * SITES * TOKENS // TOK_DEV)
    routes = jax.vmap(lambda own, number: shared_out(jax.random.fold_in(arg_keys[1], 2), own, number, TOK_DEV, EXPERTS, 1, SLOTS, 1))(routes_keys, routes_turns).reshape((STEPS, SITES, TOKENS, 1))
    hiddens = noise(arg_keys[2], (STEPS, SITES, EXPERTS, EXP_ROWS, FF_E), 1.0, 6.0, ((1, 8), (2, 4)))
    weights = noise(arg_keys[3], (SITES, EXPERTS, FF_E, D), 1.0, 6.0, ((0, 8), (1, 4)))
    tracker_offset = draw_tracker_offset(jax.random.fold_in(arg_keys[6], 71), 0)
    partner_bits = draw_partner_bits(jax.random.fold_in(arg_keys[6], 71), 0)
    return {"out_grads": out_grads, "routes": routes, "hiddens": hiddens, "weights": weights, "tracker_offset": tracker_offset, "partner_bits": partner_bits}


coef_a = 3.4445
coef_b = -4.775
coef_c = 2.0315
step_scale = 32.0
weight_hop = 4

def orthogonalize(tracked):
    frobenius = jnp.sqrt(jnp.sum(tracked * tracked))
    current = (tracked / (frobenius + 1e-07)).astype(jnp.bfloat16)
    for repeat in range(NS_ITERS):
        gram_matrix = lax.dot_general(current, current, (((1,), (1,)), ((), ())), preferred_element_type=jnp.float32).astype(jnp.bfloat16)
        squared = jnp.dot(gram_matrix, gram_matrix, preferred_element_type=jnp.float32)
        polynomial = (coef_b * gram_matrix.astype(jnp.float32) + coef_c * squared).astype(jnp.bfloat16)
        current = (coef_a * current.astype(jnp.float32) + jnp.dot(polynomial, current, preferred_element_type=jnp.float32)).astype(jnp.bfloat16)
    return current

def place_rows(gradient, routing):
    owned = (routing[:, None] == jnp.arange(EXPERTS, dtype=jnp.int32)[None, :]).astype(jnp.int32)
    earlier = jnp.cumsum(owned, axis=0) - owned
    position = lax.optimization_barrier(jnp.sum(earlier * owned, axis=1))
    target = routing * SLOTS + position
    selector = (target[None, :] == jnp.arange(EXPERTS * SLOTS, dtype=jnp.int32)[:, None]).astype(jnp.bfloat16)
    return jnp.dot(selector, gradient, preferred_element_type=jnp.float32).astype(jnp.bfloat16)

def site_gradients(inputs):
    gradient, routing, stashed = inputs
    placed = jax.vmap(place_rows)(gradient, routing)
    placed = placed.reshape(EXPERTS, EXPERTS, SLOTS, D)
    arrived = jnp.transpose(placed, (1, 0, 2, 3)).reshape(EXPERTS, EXP_ROWS, D)
    product = jnp.einsum('erf,erd->efd', stashed.astype(jnp.float32), arrived.astype(jnp.float32))
    return (product * (1.0 / math.sqrt(EXP_ROWS))).astype(jnp.bfloat16)

def partner_of(values, distance, direction):
    ahead_value = jnp.roll(values, -distance, axis=0)
    behind = jnp.roll(values, distance, axis=0)
    return jnp.where((direction == 1)[:, None, None, None], ahead_value, behind)

def reference(out_grads, routes, hiddens, weights, tracker_offset, partner_bits):
    offset = tracker_offset
    updates = jnp.zeros((SITES, EXPERTS, FF_E, D), jnp.float32)
    for round_index in range(STEPS):
        gradient = lax.map(site_gradients, (out_grads[round_index].reshape(SITES, EXPERTS, TOK_DEV, D), routes[round_index, :, :, 0].reshape(SITES, EXPERTS, TOK_DEV), hiddens[round_index]))
        distance = 2 ** round_index
        summed = offset.astype(jnp.float32) + gradient.astype(jnp.float32)
        tracked = 0.5 * (summed + partner_of(summed, distance, partner_bits[:, round_index]))
        offset = (tracked - gradient.astype(jnp.float32)).astype(jnp.bfloat16)
        ortho = lax.map(orthogonalize, tracked.reshape(SITES * EXPERTS, FF_E, D))
        updates = updates + ortho.reshape(SITES, EXPERTS, FF_E, D).astype(jnp.float32)
    moved = weights.astype(jnp.float32) - step_scale * updates
    beside_all = jnp.roll(moved, -weight_hop, axis=0) + jnp.roll(moved, weight_hop, axis=0)
    return (0.5 * moved + 0.25 * beside_all).astype(jnp.bfloat16)
```

```python
import functools
import math

import jax
import jax.numpy as jnp
from jax import lax
from jax.experimental import pallas as pl
from jax.experimental.pallas import tpu as pltpu
from jax.sharding import PartitionSpec as P

NS_ITERS = 2
CHUNKS = 4
OUT_CHUNKS = 2

coef_a = 3.4445
coef_b = -4.775
coef_c = 2.0315
step_scale = 32.0
weight_hop = 4

VMEM = pl.BlockSpec(memory_space=pltpu.VMEM)
SMEM = pl.BlockSpec(memory_space=pltpu.SMEM)


def params():
    return pltpu.CompilerParams(vmem_limit_bytes=32 * 1024 * 1024)


def dot(a, b, dims):
    return lax.dot_general(a, b, (dims, ((), ())), preferred_element_type=jnp.float32)


def newton_schulz(current):
    for repeat in range(NS_ITERS):
        gram = dot(current, current, ((1,), (1,))).astype(jnp.bfloat16)
        squared = dot(gram, gram, ((1,), (0,)))
        poly = (coef_b * gram.astype(jnp.float32) + coef_c * squared).astype(jnp.bfloat16)
        product = dot(poly, current, ((1,), (0,)))
        current = (coef_a * current.astype(jnp.float32) + product).astype(jnp.bfloat16)
    return current


def normalized(tracked):
    total = sum(jnp.sum(part * part) for part in tracked)
    scale = 1.0 / (jnp.sqrt(total) + 1e-07)
    return jnp.concatenate([(part * scale).astype(jnp.bfloat16) for part in tracked], axis=0)


def first_step_kernel(*refs):
    tracked, (weight, moved) = refs[:-2], refs[-2:]
    ortho = newton_schulz(normalized([part[...] for part in tracked]))
    moved[...] = (
        weight[...].astype(jnp.float32) - step_scale * ortho.astype(jnp.float32)
    ).astype(moved.dtype)


def second_step_kernel(chunks, flags, *refs):
    own, same, other = refs[:chunks], refs[chunks : 2 * chunks], refs[2 * chunks : 3 * chunks]
    weight, swapped_weight, moved = refs[3 * chunks :]
    use_same, is_swapped = flags[0] == 1, flags[1] == 1
    tracked = []
    for k in range(chunks):
        partner = jnp.where(use_same, same[k][...], other[k][...])
        tracked.append(0.5 * (own[k][...].astype(jnp.float32) + partner.astype(jnp.float32)))
    ortho = newton_schulz(normalized(tracked))
    base = jnp.where(is_swapped, swapped_weight[...], weight[...]).astype(jnp.float32)
    moved[...] = (base - step_scale * ortho.astype(jnp.float32)).astype(moved.dtype)


def gradient_kernel(sources, with_sum, index, *refs):
    routes, tokens = refs[0], refs[1 : 1 + sources]
    hidden = refs[1 + sources]
    rows = hidden.shape[0]
    slots = rows // sources
    count = tokens[0].shape[0]
    mine = index[0]
    earlier = (
        lax.broadcasted_iota(jnp.int32, (count, count), 0)
        < lax.broadcasted_iota(jnp.int32, (count, count), 1)
    ).astype(jnp.bfloat16)
    slot = lax.broadcasted_iota(jnp.int32, (slots, count), 0).astype(jnp.float32)
    taken = []
    for j in range(sources):
        match = (routes[j : j + 1, :] == mine).astype(jnp.float32)
        match = jnp.broadcast_to(match, (8, count))
        position = dot(match.astype(jnp.bfloat16), earlier, ((1,), (0,)))[0:1, :]
        chosen = jnp.where((slot == position) & (match[0:1, :] > 0.5), 1.0, 0.0).astype(jnp.bfloat16)
        start = pl.multiple_of((mine ^ j) * slots, slots)
        block = hidden[pl.ds(start, slots), :]
        taken.append(dot(chosen, block, ((0,), (0,))).astype(jnp.bfloat16))
    spread = jnp.concatenate(taken, axis=0)
    everything = jnp.concatenate([t[...] for t in tokens], axis=0)
    product = dot(spread, everything, ((0,), (0,)))
    grad = (product * (1.0 / math.sqrt(rows))).astype(jnp.bfloat16)
    if with_sum:
        offset, out, summed = refs[2 + sources :]
        summed[...] = (offset[...].astype(jnp.float32) + grad.astype(jnp.float32)).astype(summed.dtype)
    else:
        (out,) = refs[2 + sources :]
    out[...] = grad


def call(kernel, in_specs, out_shape, flops, moved_bytes, args):
    single = not isinstance(out_shape, (list, tuple))
    return pl.pallas_call(
        kernel,
        in_specs=in_specs,
        out_specs=VMEM if single else [VMEM] * len(out_shape),
        out_shape=out_shape,
        compiler_params=params(),
        cost_estimate=pl.CostEstimate(flops=flops, bytes_accessed=moved_bytes, transcendentals=0),
    )(*args)


def paired(out_grads, routes, hiddens, weights, tracker_offset, partner_bits):
    sites, experts = lax.axis_size("site"), lax.axis_size("expert")
    half = sites // 2
    site, expert = lax.axis_index("site"), lax.axis_index("expert")
    both = ("site", "expert")

    cross = []
    for s in range(half):
        for e in range(1, experts, 2):
            here, there = s * experts + e, (s + half) * experts + e - 1
            cross += [(here, there), (there, here)]
    mates = [(e, e ^ 1) for e in range(experts)]
    beside = [(s, s ^ 1) for s in range(sites)]
    helpers = [(s, (s + 2) % sites if s % 2 else (s - 2) % sites) for s in range(sites)]
    within = [(s, s // half * half + (s + 2) % half) for s in range(sites)]

    weight, offset = weights[0, 0], tracker_offset[0, 0]
    stashed = hiddens[:, 0, 0]
    tokens, routing = out_grads[:, 0], routes[:, 0, :, 0]
    steps = tokens.shape[0]
    fan_rows, features = weight.shape
    bits = partner_bits[0]

    is_swapped = (site < half) == (expert % 2 == 1)
    beside_bits = lax.ppermute(bits, "site", beside)
    cross_bits = lax.ppermute(bits, both, cross)
    send_own = jnp.where(site % 2 == 1, beside_bits[0] == 1, beside_bits[0] == 0)
    problem = site % half + half * (expert % 2)
    second_bit = jnp.where(is_swapped, cross_bits[1], bits[1])
    wanted = jnp.where(second_bit == 1, problem + 2, problem - 2 + sites) % sites
    use_same = wanted == (site + half - 2) % half + half * (expert % 2)

    gathered = [[tokens[k]] for k in range(steps)]
    named = [routing]
    level = experts // 2
    order = []
    while level >= 1:
        order.append(level)
        level //= 2
    have = [0]
    for level in order:
        hop = [(e, e ^ level) for e in range(experts)]
        named = named + [lax.ppermute(r, "expert", hop) for r in named]
        for k in range(steps):
            gathered[k] = gathered[k] + [lax.ppermute(t, "expert", hop) for t in gathered[k]]
        have = have + [h ^ level for h in have]
    rank = [have.index(j) for j in range(experts)]
    named = jnp.stack([named[i] for i in rank])
    index = expert.astype(jnp.int32)[None]

    shape = jax.ShapeDtypeStruct((fan_rows, features), jnp.bfloat16)
    grads = []
    for k in range(steps):
        args = [index, named[:, k]] + [gathered[k][i] for i in rank] + [stashed[k]]
        if k == 0:
            args.append(offset)
        made = call(
            functools.partial(gradient_kernel, experts, k == 0),
            [SMEM] + [VMEM] * (len(args) - 1),
            [shape, shape] if k == 0 else shape,
            2 * fan_rows * features * experts * tokens.shape[1],
            4 * fan_rows * features,
            args,
        )
        if k == 0:
            grad, summed = made
            grads.append(grad)
        else:
            grads.append(made)

    rows = fan_rows // CHUNKS
    parts = [slice(i * rows, (i + 1) * rows) for i in range(CHUNKS)]
    own = [summed[p] for p in parts]
    fetched = [lax.ppermute(o, "site", helpers) for o in own]
    tracked, second = [], []
    for i, p in enumerate(parts):
        chosen = jnp.where(send_own, own[i], fetched[i])
        partner = lax.ppermute(chosen, "site", beside).astype(jnp.float32)
        grad = grads[0][p].astype(jnp.float32)
        now = 0.5 * ((offset[p].astype(jnp.float32) + grad) + partner)
        tracked.append(now)
        later = (now - grad).astype(jnp.bfloat16).astype(jnp.float32)
        second.append((later + grads[1][p].astype(jnp.float32)).astype(jnp.bfloat16))
    mine, same, other = [], [], []
    for i in range(CHUNKS):
        arrived = lax.ppermute(second[i], both, cross)
        value = jnp.where(is_swapped, arrived, second[i])
        mine.append(value)
        same.append(lax.ppermute(value, "site", within))
        other.append(lax.ppermute(same[-1], "expert", mates))

    cost = NS_ITERS * 2 * (2 * fan_rows * fan_rows * features + fan_rows**3)
    moved = call(
        first_step_kernel, [VMEM] * (CHUNKS + 1), shape, cost, 8 * fan_rows * features, tracked + [weight]
    )
    swapped_moved = lax.ppermute(moved, both, cross)
    flags = jnp.stack([use_same, is_swapped]).astype(jnp.int32)
    moved = call(
        functools.partial(second_step_kernel, CHUNKS),
        [SMEM] + [VMEM] * (3 * CHUNKS + 2),
        shape,
        cost,
        12 * fan_rows * features,
        [flags] + mine + same + other + [moved, swapped_moved],
    )
    results = []
    rows = fan_rows // OUT_CHUNKS
    for i in range(OUT_CHUNKS):
        part = moved[i * rows : (i + 1) * rows]
        mate = lax.ppermute(part, "expert", mates).astype(jnp.float32)
        result = (0.5 * part.astype(jnp.float32) + 0.25 * (mate + mate)).astype(jnp.bfloat16)
        back = lax.ppermute(result, both, cross)
        results.append(jnp.where(is_swapped, back, result))
    return jnp.concatenate(results, axis=0)[None, None]


def from_behind(block, axis, distance):
    devices = range(lax.axis_size(axis))
    route = [((i - distance) % len(devices), i) for i in devices]
    return lax.ppermute(block, axis, route)


def orthogonalize(tracked):
    frobenius = jnp.sqrt(jnp.sum(tracked * tracked))
    return newton_schulz((tracked / (frobenius + 1e-07)).astype(jnp.bfloat16))


def place_rows(gradient, routing, experts, slot_count):
    owned = (routing[:, None] == jnp.arange(experts, dtype=jnp.int32)[None, :]).astype(jnp.int32)
    earlier = jnp.cumsum(owned, axis=0) - owned
    position = jnp.sum(earlier * owned, axis=1)
    target = routing * slot_count + position
    selector = (
        target[None, :] == jnp.arange(experts * slot_count, dtype=jnp.int32)[:, None]
    ).astype(jnp.bfloat16)
    placed = dot(selector, gradient, ((1,), (0,))).astype(jnp.bfloat16)
    return placed.reshape(experts, slot_count, gradient.shape[1])


def general(out_grads, routes, hiddens, weights, tracker_offset, partner_bits):
    experts = lax.axis_size("expert")
    stashed = hiddens[:, 0, 0]
    steps, slot_rows = stashed.shape[:2]
    slot_count = slot_rows // experts
    direction = partner_bits[0]
    weight, offset = weights[0, 0], tracker_offset[0, 0]
    placed = [place_rows(out_grads[k, 0], routes[k, 0, :, 0], experts, slot_count) for k in range(steps)]
    arrived = lax.all_to_all(jnp.stack(placed), "expert", split_axis=1, concat_axis=1, tiled=True)
    updates = jnp.zeros(weight.shape, jnp.float32)
    for k in range(steps):
        product = dot(stashed[k], arrived[k].reshape(slot_rows, -1), ((0,), (0,)))
        gradient = (product * (1.0 / math.sqrt(slot_rows))).astype(jnp.bfloat16).astype(jnp.float32)
        summed = offset.astype(jnp.float32) + gradient
        sent = summed.astype(jnp.bfloat16)
        distance = 2**k
        partner = jnp.where(
            direction[k] == 1,
            from_behind(sent, "site", -distance),
            from_behind(sent, "site", distance),
        )
        tracked = 0.5 * (summed + partner.astype(jnp.float32))
        offset = (tracked - gradient).astype(jnp.bfloat16)
        updates = updates + orthogonalize(tracked).astype(jnp.float32)
    updated = weight.astype(jnp.float32) - step_scale * updates
    sent = updated.astype(jnp.bfloat16)
    beside = from_behind(sent, "site", -weight_hop).astype(jnp.float32) + from_behind(
        sent, "site", weight_hop
    ).astype(jnp.float32)
    return (0.5 * updated + 0.25 * beside).astype(jnp.bfloat16)[None, None]


def solution(mesh):
    in_specs = (
        P(None, "site", "expert", None),
        P(None, "site", "expert", None),
        P(None, "site", "expert", None, None),
        P("site", "expert", None, None),
        P("site", "expert", None, None),
        P("site", None),
    )
    out_specs = P("site", "expert", None, None)
    sites, experts = mesh.shape["site"], mesh.shape["expert"]
    pairs = sites == 2 * weight_hop and experts in (2, 4)
    local = paired if pairs else general
    return jax.shard_map(local, mesh=mesh, in_specs=in_specs, out_specs=out_specs, check_vma=False)
```

```python
import functools
import math

import jax
import jax.numpy as jnp
from jax import lax
from jax.experimental import pallas as pl
from jax.experimental.pallas import tpu as pltpu
from jax.sharding import PartitionSpec as P

NS_ITERS = 2
CHUNKS = 2
SERIAL_X = False
LAG_X = 9
SERIAL_T = True
LAG_T = 9
SERIAL_W = True
NS_AFTER = 0
GATE = False
VMEM_LIMIT = 32 * 1024 * 1024

coef_a = 3.4445
coef_b = -4.775
coef_c = 2.0315
step_scale = 32.0
weight_hop = 4

ANY = pl.BlockSpec(memory_space=pl.ANY)
VMEM = pl.BlockSpec(memory_space=pltpu.VMEM)


def dot(a, b, dims):
    return lax.dot_general(a, b, (dims, ((), ())), preferred_element_type=jnp.float32)


def newton_schulz(current):
    for repeat in range(NS_ITERS):
        gram = dot(current, current, ((1,), (1,))).astype(jnp.bfloat16)
        squared = dot(gram, gram, ((1,), (0,)))
        poly = (coef_b * gram.astype(jnp.float32) + coef_c * squared).astype(jnp.bfloat16)
        product = dot(poly, current, ((1,), (0,)))
        current = (coef_a * current.astype(jnp.float32) + product).astype(jnp.bfloat16)
    return current


def normalized(tracked):
    total = sum(jnp.sum(part * part) for part in tracked)
    scale = 1.0 / (jnp.sqrt(total) + 1e-07)
    return jnp.concatenate([(part * scale).astype(jnp.bfloat16) for part in tracked], axis=0)


def first_step_kernel(chunks, *refs):
    offset, grads, partners = refs[0], refs[1 : 1 + chunks], refs[1 + chunks : 1 + 2 * chunks]
    weight, moved = refs[1 + 2 * chunks :]
    rows = grads[0].shape[0]
    tracked = []
    for k in range(chunks):
        own = offset[k * rows : (k + 1) * rows, :].astype(jnp.float32) + grads[k][...].astype(jnp.float32)
        tracked.append(0.5 * (own + partners[k][...].astype(jnp.float32)))
    ortho = newton_schulz(normalized(tracked))
    moved[...] = (
        weight[...].astype(jnp.float32) - step_scale * ortho.astype(jnp.float32)
    ).astype(moved.dtype)


def second_step_kernel(chunks, flag, *refs):
    own, same, other = refs[:chunks], refs[chunks : 2 * chunks], refs[2 * chunks : 3 * chunks]
    (ortho,) = refs[3 * chunks :]
    use_same = flag[0:1, 0:1] == 1
    tracked = []
    for k in range(chunks):
        partner = jnp.where(use_same, same[k][...].astype(jnp.float32), other[k][...].astype(jnp.float32))
        tracked.append(0.5 * (own[k][...].astype(jnp.float32) + partner))
    ortho[...] = newton_schulz(normalized(tracked))


def gradient_kernel(sources, with_sum, *refs):
    tokens, hidden, refs = refs[:sources], refs[sources], refs[sources + 1 :]
    rows = hidden.shape[0]
    slots = rows // sources
    count = tokens[0].shape[0] - 16
    mine = lax.axis_index("expert")
    earlier = (
        lax.broadcasted_iota(jnp.int32, (count, count), 0)
        < lax.broadcasted_iota(jnp.int32, (count, count), 1)
    ).astype(jnp.bfloat16)
    slot = lax.broadcasted_iota(jnp.int32, (slots, count), 0).astype(jnp.float32)
    taken = []
    for j in range(sources):
        named = tokens[j][count : count + 16, :count].astype(jnp.float32)
        match = jnp.where(named == mine.astype(jnp.float32), 1.0, 0.0)
        position = dot(match.astype(jnp.bfloat16), earlier, ((1,), (0,)))[0:1, :]
        chosen = jnp.where((slot == position) & (match[0:1, :] > 0.5), 1.0, 0.0).astype(jnp.bfloat16)
        start = pl.multiple_of((mine ^ j) * slots, slots)
        taken.append(dot(chosen, hidden[pl.ds(start, slots), :], ((0,), (0,))).astype(jnp.bfloat16))
    spread = jnp.concatenate(taken, axis=0)
    everything = jnp.concatenate([t[:count, :] for t in tokens], axis=0)
    product = dot(spread, everything, ((0,), (0,)))
    grad = (product * (1.0 / math.sqrt(rows))).astype(jnp.bfloat16)
    if with_sum:
        offset, refs = refs[0], refs[1:]
        summed = (offset[...].astype(jnp.float32) + grad.astype(jnp.float32)).astype(jnp.bfloat16)
        refs, sums = refs[: len(refs) // 2], refs[len(refs) // 2 :]
    depth = refs[0].shape[0]
    for k, out in enumerate(refs):
        out[...] = grad[k * depth : (k + 1) * depth, :]
        if with_sum:
            sums[k][...] = summed[k * depth : (k + 1) * depth, :]


def call(kernel, operands, out_shapes, flops):
    arrays = [a[0] if isinstance(a, tuple) else a for a in operands]
    fetched = {i: a[1] for i, a in enumerate(operands) if isinstance(a, tuple)}
    shapes = [a.shape if fetched.get(i) is None else a.shape[1:] for i, a in enumerate(arrays)]
    count, results, copied = len(arrays), len(out_shapes), list(fetched)

    def body(*refs):
        sources, targets = list(refs[:count]), refs[count : count + results]
        copies = []
        for n, i in enumerate(copied):
            source = sources[i] if fetched[i] is None else sources[i].at[fetched[i]]
            buffer = refs[count + results + n]
            copies.append(pltpu.make_async_copy(source, buffer, refs[-1].at[n]))
            sources[i] = buffer
        for copy in copies:
            copy.start()
        for copy in copies:
            copy.wait()
        kernel(*sources, *targets)

    moved = sum(math.prod(s) * a.dtype.itemsize for s, a in zip(shapes, arrays))
    moved += sum(math.prod(s.shape) * s.dtype.itemsize for s in out_shapes)
    return pl.pallas_call(
        body,
        in_specs=[ANY if i in fetched else VMEM for i in range(count)],
        out_specs=[VMEM] * results,
        out_shape=out_shapes,
        scratch_shapes=[pltpu.VMEM(shapes[i], arrays[i].dtype) for i in copied]
        + [pltpu.SemaphoreType.DMA((max(1, len(copied)),))],
        compiler_params=pltpu.CompilerParams(vmem_limit_bytes=VMEM_LIMIT),
        cost_estimate=pl.CostEstimate(flops=flops, bytes_accessed=moved, transcendentals=0),
    )(*arrays)


def after(value, earlier):
    return lax.optimization_barrier((value, earlier))[0]


def paired(out_grads, routes, hiddens, weights, tracker_offset, partner_bits):
    sites, experts = lax.axis_size("site"), lax.axis_size("expert")
    half = sites // 2
    site, expert = lax.axis_index("site"), lax.axis_index("expert")
    both = ("site", "expert")

    cross, kept, from_mate, lent = [], [], [], []
    for s in range(half):
        for e in range(0, experts, 2):
            low, high = s * experts + e, (s + half) * experts + e
            cross += [(low + 1, high), (high, low + 1)]
            kept += [(low, low), (high + 1, high + 1)]
            from_mate += [(low, low + 1), (high + 1, high)]
            lent += [(high, low), (low + 1, high + 1)]
    swap = cross + kept
    mates = [(e, e ^ 1) for e in range(experts)]
    beside = [(s, s ^ 1) for s in range(sites)]
    helpers = [(s, (s + 2) % sites if s % 2 else (s - 2) % sites) for s in range(sites)]
    within = [(s, s // half * half + (s + 2) % half) for s in range(sites)]

    weight, offset = weights[0, 0], tracker_offset[0, 0]
    stashed = hiddens[:, 0, 0]
    tokens, routing = out_grads[:, 0], routes[:, 0, :, 0]
    steps = tokens.shape[0]
    fan_rows, features = weight.shape
    bits = partner_bits[0]
    is_swapped = (site < half) == (expert % 2 == 1)

    beside_bits = lax.ppermute(bits, "site", beside)
    swap_bits = lax.ppermute(bits, both, swap)
    send_own = jnp.where(site % 2 == 1, beside_bits[0] == 1, beside_bits[0] == 0)
    problem = site % half + half * (expert % 2)
    wanted = jnp.where(swap_bits[1] == 1, problem + 2, problem - 2 + sites) % sites
    use_same = wanted == (site + half - 2) % half + half * (expert % 2)
    use_same = jnp.full((8, 128), use_same.astype(jnp.int32))

    count = tokens.shape[1]
    named = routing.astype(jnp.bfloat16).reshape(steps, 1, count)
    named = jnp.pad(named, ((0, 0), (0, 15), (0, features - count)))
    gathered = [{0: jnp.concatenate([tokens[k], named[k]], axis=0)} for k in range(steps)]
    top = experts // 2
    for k in range(steps):
        level = top
        if k > 0:
            gathered[k][0] = after(gathered[k][0], gathered[k - 1][top])
        while level >= 1:
            hop = [(e, e ^ level) for e in range(experts)]
            gathered[k].update({j ^ level: lax.ppermute(t, "expert", hop) for j, t in gathered[k].items()})
            if k == 0 and level == top:
                gathered[k][top], (send_own, use_same) = lax.optimization_barrier(
                    (gathered[k][top], (send_own, use_same))
                )
            level //= 2

    rows = fan_rows // CHUNKS
    parts = [slice(i * rows, (i + 1) * rows) for i in range(CHUNKS)]
    chunk = [jax.ShapeDtypeStruct((rows, features), jnp.bfloat16)] * CHUNKS
    whole = [jax.ShapeDtypeStruct((fan_rows, features), jnp.bfloat16)]
    cost = 2 * fan_rows * features * experts * count
    operands = [gathered[0][j] for j in range(experts)] + [(stashed, 0), (offset, None)]
    made = call(functools.partial(gradient_kernel, experts, True), operands, chunk * 2, cost)
    first, own = made[:CHUNKS], list(made[CHUNKS:])
    fetched = [lax.ppermute(o, "site", helpers) for o in own]
    operands = [gathered[1][j] for j in range(experts)] + [(stashed, 1)]
    last = call(functools.partial(gradient_kernel, experts, False), operands, chunk, cost)

    chosen, partners, second, mine, same, other = [], [], [], [], [], []
    for i in range(CHUNKS):
        arrived = after(fetched[i], last[0] if i == 0 else chosen[i - 1])
        chosen.append(jnp.where(send_own, own[i], arrived))
    for i in range(CHUNKS):
        if i > 0:
            chosen[i] = after(chosen[i], partners[i - 1]) if SERIAL_X else chosen[i]
        if i >= LAG_X:
            chosen[i] = after(chosen[i], mine[i - LAG_X])
        partners.append(lax.ppermute(chosen[i], "site", beside))
        partner = partners[i] if i == 0 else after(partners[i], second[i - 1])
        grad = first[i].astype(jnp.float32)
        tracked = 0.5 * ((offset[parts[i]].astype(jnp.float32) + grad) + partner.astype(jnp.float32))
        later = (tracked - grad).astype(jnp.bfloat16).astype(jnp.float32)
        second.append((later + last[i].astype(jnp.float32)).astype(jnp.bfloat16))
        if i > 0 and SERIAL_T:
            second[i] = after(second[i], mine[i - 1])
        if i >= LAG_T:
            second[i] = after(second[i], same[i - LAG_T])
        mine.append(lax.ppermute(second[i], both, swap))
        if i < CHUNKS - 1:
            value = mine[i]
            if i > 0 and SERIAL_W:
                value = after(value, same[i - 1])
            same.append(lax.ppermute(value, "site", within))

    cost = NS_ITERS * 2 * (2 * fan_rows * fan_rows * features + fan_rows**3)
    held = [after(partners[-1], mine[NS_AFTER])]
    (moved,) = call(
        functools.partial(first_step_kernel, CHUNKS),
        [(offset, None), *first, *partners[:-1], *held, (weight, None)],
        whole,
        cost,
    )
    value = after(mine[-1], moved)
    if SERIAL_W:
        value = after(value, same[-1])
    same.append(lax.ppermute(value, "site", within))
    other = [lax.ppermute(value, "expert", mates) for value in same]
    borrowed = lax.ppermute(after(moved, mine[-1]), both, lent)
    if GATE:
        other[-1] = after(other[-1], borrowed)
    shared = (moved.astype(jnp.float32) + borrowed.astype(jnp.float32)).astype(jnp.bfloat16)
    given = lax.ppermute(shared, both, from_mate)
    shared = jnp.where(is_swapped, given, shared)
    (ortho,) = call(
        functools.partial(second_step_kernel, CHUNKS), [use_same, *mine, *same, *other], whole, cost
    )
    paired_ortho = lax.ppermute(ortho, "expert", mates)
    result = 0.5 * shared.astype(jnp.float32) - 0.5 * step_scale * (
        ortho.astype(jnp.float32) + paired_ortho.astype(jnp.float32)
    )
    return lax.ppermute(result.astype(jnp.bfloat16)[None, None], both, swap)


def from_behind(block, axis, distance):
    devices = range(lax.axis_size(axis))
    route = [((i - distance) % len(devices), i) for i in devices]
    return lax.ppermute(block, axis, route)


def orthogonalize(tracked):
    frobenius = jnp.sqrt(jnp.sum(tracked * tracked))
    return newton_schulz((tracked / (frobenius + 1e-07)).astype(jnp.bfloat16))


def place_rows(gradient, routing, experts, slot_count):
    owned = (routing[:, None] == jnp.arange(experts, dtype=jnp.int32)[None, :]).astype(jnp.int32)
    earlier = jnp.cumsum(owned, axis=0) - owned
    position = jnp.sum(earlier * owned, axis=1)
    target = routing * slot_count + position
    selector = (
        target[None, :] == jnp.arange(experts * slot_count, dtype=jnp.int32)[:, None]
    ).astype(jnp.bfloat16)
    placed = dot(selector, gradient, ((1,), (0,))).astype(jnp.bfloat16)
    return placed.reshape(experts, slot_count, gradient.shape[1])


def general(out_grads, routes, hiddens, weights, tracker_offset, partner_bits):
    experts = lax.axis_size("expert")
    stashed = hiddens[:, 0, 0]
    steps, slot_rows = stashed.shape[:2]
    slot_count = slot_rows // experts
    direction = partner_bits[0]
    weight, offset = weights[0, 0], tracker_offset[0, 0]
    placed = [place_rows(out_grads[k, 0], routes[k, 0, :, 0], experts, slot_count) for k in range(steps)]
    arrived = lax.all_to_all(jnp.stack(placed), "expert", split_axis=1, concat_axis=1, tiled=True)
    updates = jnp.zeros(weight.shape, jnp.float32)
    for k in range(steps):
        product = dot(stashed[k], arrived[k].reshape(slot_rows, -1), ((0,), (0,)))
        gradient = (product * (1.0 / math.sqrt(slot_rows))).astype(jnp.bfloat16).astype(jnp.float32)
        summed = offset.astype(jnp.float32) + gradient
        sent = summed.astype(jnp.bfloat16)
        distance = 2**k
        partner = jnp.where(
            direction[k] == 1,
            from_behind(sent, "site", -distance),
            from_behind(sent, "site", distance),
        )
        tracked = 0.5 * (summed + partner.astype(jnp.float32))
        offset = (tracked - gradient).astype(jnp.bfloat16)
        updates = updates + orthogonalize(tracked).astype(jnp.float32)
    updated = weight.astype(jnp.float32) - step_scale * updates
    sent = updated.astype(jnp.bfloat16)
    beside = from_behind(sent, "site", -weight_hop).astype(jnp.float32) + from_behind(
        sent, "site", weight_hop
    ).astype(jnp.float32)
    return (0.5 * updated + 0.25 * beside).astype(jnp.bfloat16)[None, None]


def solution(mesh):
    in_specs = (
        P(None, "site", "expert", None),
        P(None, "site", "expert", None),
        P(None, "site", "expert", None, None),
        P("site", "expert", None, None),
        P("site", "expert", None, None),
        P("site", None),
    )
    out_specs = P("site", "expert", None, None)
    sites, experts = mesh.shape["site"], mesh.shape["expert"]
    pairs = sites == 2 * weight_hop and experts in (2, 4)
    local = paired if pairs else general
    return jax.shard_map(local, mesh=mesh, in_specs=in_specs, out_specs=out_specs, check_vma=False)
```

```python
import functools
import math

import jax
import jax.numpy as jnp
from jax import lax
from jax.experimental import pallas as pl
from jax.experimental.pallas import tpu as pltpu
from jax.sharding import PartitionSpec as P

NS_ITERS = 2
CHUNKS = 2
BLOCKS = 2
SERIAL_X = False
LAG_X = 9
LAG_S = 9
SERIAL_T = False
LAG_T = 9
SERIAL_W = True
NS_AFTER = 0
GATE = False
VMEM_LIMIT = 32 * 1024 * 1024

coef_a = 3.4445
coef_b = -4.775
coef_c = 2.0315
step_scale = 32.0
weight_hop = 4

ANY = pl.BlockSpec(memory_space=pl.ANY)
VMEM = pl.BlockSpec(memory_space=pltpu.VMEM)


def dot(a, b, dims):
    return lax.dot_general(a, b, (dims, ((), ())), preferred_element_type=jnp.float32)


def newton_schulz(current):
    for repeat in range(NS_ITERS):
        gram = dot(current, current, ((1,), (1,))).astype(jnp.bfloat16)
        squared = dot(gram, gram, ((1,), (0,)))
        poly = (coef_b * gram.astype(jnp.float32) + coef_c * squared).astype(jnp.bfloat16)
        product = dot(poly, current, ((1,), (0,)))
        current = (coef_a * current.astype(jnp.float32) + product).astype(jnp.bfloat16)
    return current


def normalized(tracked):
    total = sum(jnp.sum(part * part) for part in tracked)
    scale = 1.0 / (jnp.sqrt(total) + 1e-07)
    return jnp.concatenate([(part * scale).astype(jnp.bfloat16) for part in tracked], axis=0)


def first_step_kernel(chunks, *refs):
    offset, grads, partners = refs[0], refs[1 : 1 + chunks], refs[1 + chunks : 1 + 2 * chunks]
    weight, moved = refs[1 + 2 * chunks :]
    start, tracked = 0, []
    for k in range(chunks):
        part = slice(start, start + grads[k].shape[0])
        start = part.stop
        own = offset[part, :].astype(jnp.float32) + grads[k][...].astype(jnp.float32)
        tracked.append(0.5 * (own + partners[k][...].astype(jnp.float32)))
    ortho = newton_schulz(normalized(tracked))
    moved[...] = (
        weight[...].astype(jnp.float32) - step_scale * ortho.astype(jnp.float32)
    ).astype(moved.dtype)


def second_step_kernel(chunks, bits, *refs):
    own, same, other = refs[:chunks], refs[chunks : 2 * chunks], refs[2 * chunks : 3 * chunks]
    blocks = refs[3 * chunks :]
    sites, site, core = lax.axis_size("site"), lax.axis_index("site"), lax.axis_index("expert") % 2
    half = sites // 2
    problem, source = site % half + half * core, (site + half - 2) % half + half * core
    ahead_same = ((problem + 2) % sites == source).astype(jnp.int32)
    use_same = bits[0:1, 1:2] == ahead_same
    tracked = []
    for k in range(chunks):
        partner = jnp.where(use_same, same[k][...].astype(jnp.float32), other[k][...].astype(jnp.float32))
        tracked.append(0.5 * (own[k][...].astype(jnp.float32) + partner))
    ortho = newton_schulz(normalized(tracked))
    rows = blocks[0].shape[0]
    for k, block in enumerate(blocks):
        block[...] = ortho[k * rows : (k + 1) * rows, :]


def last_kernel(blocks, ready, *refs):
    back, out, buffer, semaphores = refs[:blocks], *refs[blocks:]
    rows = back[0].shape[0]
    copies = []
    for k in range(blocks):
        part = pl.ds(k * rows, rows)
        value = ready[part, :].astype(jnp.float32) + 0.5 * back[k][...].astype(jnp.float32)
        buffer[part, :] = value.astype(buffer.dtype)
        copies.append(pltpu.make_async_copy(buffer.at[part], out.at[0, 0, part], semaphores.at[k]))
        copies[-1].start()
    for copy in copies:
        copy.wait()


def gradient_kernel(sources, with_sum, *refs):
    tokens, hidden, refs = refs[:sources], refs[sources], refs[sources + 1 :]
    rows = hidden.shape[0]
    slots = rows // sources
    count = tokens[0].shape[0] - 16
    mine = lax.axis_index("expert")
    earlier = (
        lax.broadcasted_iota(jnp.int32, (count, count), 0)
        < lax.broadcasted_iota(jnp.int32, (count, count), 1)
    ).astype(jnp.bfloat16)
    slot = lax.broadcasted_iota(jnp.int32, (slots, count), 0).astype(jnp.float32)
    taken = []
    for j in range(sources):
        named = tokens[j][count : count + 16, :count].astype(jnp.float32)
        match = jnp.where(named == mine.astype(jnp.float32), 1.0, 0.0)
        position = dot(match.astype(jnp.bfloat16), earlier, ((1,), (0,)))[0:1, :]
        chosen = jnp.where((slot == position) & (match[0:1, :] > 0.5), 1.0, 0.0).astype(jnp.bfloat16)
        start = pl.multiple_of((mine ^ j) * slots, slots)
        taken.append(dot(chosen, hidden[pl.ds(start, slots), :], ((0,), (0,))).astype(jnp.bfloat16))
    spread = jnp.concatenate(taken, axis=0)
    everything = jnp.concatenate([t[:count, :] for t in tokens], axis=0)
    product = dot(spread, everything, ((0,), (0,)))
    grad = (product * (1.0 / math.sqrt(rows))).astype(jnp.bfloat16)
    if with_sum:
        offset, refs = refs[0], refs[1:]
        summed = (offset[...].astype(jnp.float32) + grad.astype(jnp.float32)).astype(jnp.bfloat16)
        refs, sums = refs[: len(refs) // 2], refs[len(refs) // 2 :]
    start = 0
    for k, out in enumerate(refs):
        part = slice(start, start + out.shape[0])
        start = part.stop
        out[...] = grad[part, :]
        if with_sum:
            sums[k][...] = summed[part, :]


def call(kernel, operands, out_shapes, flops):
    arrays = [a[0] if isinstance(a, tuple) else a for a in operands]
    fetched = {i: a[1] for i, a in enumerate(operands) if isinstance(a, tuple)}
    shapes = [a.shape if fetched.get(i) is None else a.shape[1:] for i, a in enumerate(arrays)]
    count, results, copied = len(arrays), len(out_shapes), list(fetched)

    def body(*refs):
        sources, targets = list(refs[:count]), refs[count : count + results]
        copies = []
        for n, i in enumerate(copied):
            source = sources[i] if fetched[i] is None else sources[i].at[fetched[i]]
            buffer = refs[count + results + n]
            copies.append(pltpu.make_async_copy(source, buffer, refs[-1].at[n]))
            sources[i] = buffer
        for copy in copies:
            copy.start()
        for copy in copies:
            copy.wait()
        kernel(*sources, *targets)

    moved = sum(math.prod(s) * a.dtype.itemsize for s, a in zip(shapes, arrays))
    moved += sum(math.prod(s.shape) * s.dtype.itemsize for s in out_shapes)
    return pl.pallas_call(
        body,
        in_specs=[ANY if i in fetched else VMEM for i in range(count)],
        out_specs=[VMEM] * results,
        out_shape=out_shapes,
        scratch_shapes=[pltpu.VMEM(shapes[i], arrays[i].dtype) for i in copied]
        + [pltpu.SemaphoreType.DMA((max(1, len(copied)),))],
        compiler_params=pltpu.CompilerParams(vmem_limit_bytes=VMEM_LIMIT),
        cost_estimate=pl.CostEstimate(flops=flops, bytes_accessed=moved, transcendentals=0),
    )(*arrays)


def after(value, earlier):
    return lax.optimization_barrier((value, earlier))[0]


def paired(out_grads, routes, hiddens, weights, tracker_offset, partner_bits):
    sites, experts = lax.axis_size("site"), lax.axis_size("expert")
    half = sites // 2
    site, expert = lax.axis_index("site"), lax.axis_index("expert")
    both = ("site", "expert")

    cross, kept, to_mate, lent, returned = [], [], [], [], []
    for s in range(half):
        for e in range(0, experts, 2):
            low, high = s * experts + e, (s + half) * experts + e
            cross += [(low + 1, high), (high, low + 1)]
            kept += [(low, low), (high + 1, high + 1)]
            to_mate += [(low + 1, low), (high, high + 1)]
            lent += [(high, low), (low + 1, high + 1)]
            returned += [(low, high), (high + 1, low + 1)]
    swap = cross + kept
    mates = [(e, e ^ 1) for e in range(experts)]
    beside = [(s, s ^ 1) for s in range(sites)]
    helpers = [(s, (s + 2) % sites if s % 2 else (s - 2) % sites) for s in range(sites)]
    within = [(s, s // half * half + (s + 2) % half) for s in range(sites)]

    weight, offset = weights[0, 0], tracker_offset[0, 0]
    stashed = hiddens[:, 0, 0]
    tokens, routing = out_grads[:, 0], routes[:, 0, :, 0]
    steps = tokens.shape[0]
    fan_rows, features = weight.shape
    bits = partner_bits[0]
    is_swapped = (site < half) == (expert % 2 == 1)

    beside_bits = lax.ppermute(bits, "site", beside)
    swap_bits = lax.ppermute(bits, both, swap)
    send_own = beside_bits.reshape(1, -1)[:, 0:1] == site % 2
    swap_bits = swap_bits.reshape(1, -1)

    count = tokens.shape[1]
    named = routing.astype(jnp.bfloat16).reshape(steps, 1, count)
    named = jnp.pad(named, ((0, 0), (0, 15), (0, features - count)))
    gathered = [{0: jnp.concatenate([tokens[k], named[k]], axis=0)} for k in range(steps)]
    top = experts // 2
    for k in range(steps):
        level = top
        if k > 0:
            gathered[k][0] = after(gathered[k][0], gathered[k - 1][top])
        while level >= 1:
            hop = [(e, e ^ level) for e in range(experts)]
            gathered[k].update({j ^ level: lax.ppermute(t, "expert", hop) for j, t in gathered[k].items()})
            if k == 0 and level == top:
                gathered[k][top], (send_own, swap_bits) = lax.optimization_barrier(
                    (gathered[k][top], (send_own, swap_bits))
                )
            level //= 2

    edges = [fan_rows // 16 * i // CHUNKS * 16 for i in range(CHUNKS)] + [fan_rows]
    parts = [slice(low, high) for low, high in zip(edges, edges[1:])]
    chunk = [jax.ShapeDtypeStruct((p.stop - p.start, features), jnp.bfloat16) for p in parts]
    whole = [jax.ShapeDtypeStruct((fan_rows, features), jnp.bfloat16)]
    cost = 2 * fan_rows * features * experts * count
    operands = [gathered[0][j] for j in range(experts)] + [(stashed, 0), (offset, None)]
    made = call(functools.partial(gradient_kernel, experts, True), operands, chunk * 2, cost)
    first, own = made[:CHUNKS], list(made[CHUNKS:])
    fetched = [lax.ppermute(o, "site", helpers) for o in own]
    operands = [gathered[1][j] for j in range(experts)] + [(stashed, 1)]
    last = call(functools.partial(gradient_kernel, experts, False), operands, chunk, cost)

    chosen, partners, second, mine, same, other = [], [], [], [], [], []
    for i in range(CHUNKS):
        arrived = after(fetched[i], last[0] if i == 0 else chosen[i - 1])
        chosen.append(jnp.where(send_own, own[i], arrived))
    for i in range(CHUNKS):
        if i > 0:
            chosen[i] = after(chosen[i], partners[i - 1]) if SERIAL_X else chosen[i]
        if i >= LAG_S:
            chosen[i] = after(chosen[i], second[i - LAG_S])
        if i >= LAG_X:
            chosen[i] = after(chosen[i], mine[i - LAG_X])
        partners.append(lax.ppermute(chosen[i], "site", beside))
        partner = partners[i] if i == 0 else after(partners[i], second[i - 1])
        grad = first[i].astype(jnp.float32)
        tracked = 0.5 * ((offset[parts[i]].astype(jnp.float32) + grad) + partner.astype(jnp.float32))
        later = (tracked - grad).astype(jnp.bfloat16).astype(jnp.float32)
        second.append((later + last[i].astype(jnp.float32)).astype(jnp.bfloat16))
        if i > 0 and SERIAL_T:
            second[i] = after(second[i], mine[i - 1])
        if i >= LAG_T:
            second[i] = after(second[i], same[i - LAG_T])
        mine.append(lax.ppermute(second[i], both, swap))
        if i < CHUNKS - 1:
            value = mine[i]
            if i > 0 and SERIAL_W:
                value = after(value, same[i - 1])
            same.append(lax.ppermute(value, "site", within))

    cost = NS_ITERS * 2 * (2 * fan_rows * fan_rows * features + fan_rows**3)
    held = [after(partners[-1], mine[NS_AFTER])]
    (moved,) = call(
        functools.partial(first_step_kernel, CHUNKS),
        [(offset, None), *first, *partners[:-1], *held, (weight, None)],
        whole,
        cost,
    )
    value = after(mine[-1], moved)
    if SERIAL_W:
        value = after(value, same[-1])
    same.append(lax.ppermute(value, "site", within))
    other = [lax.ppermute(value, "expert", mates) for value in same]
    borrowed = lax.ppermute(after(moved, mine[-1]), both, lent)
    if GATE:
        other[-1] = after(other[-1], borrowed)
    block_rows = fan_rows // BLOCKS
    block = [jax.ShapeDtypeStruct((block_rows, features), jnp.bfloat16)] * BLOCKS
    ortho = list(call(functools.partial(second_step_kernel, CHUNKS), [swap_bits, *mine, *same, *other], block, cost))
    ortho[0] = after(ortho[0], borrowed)
    paired_ortho = [lax.ppermute(o, both, to_mate) for o in ortho]
    sent = []
    for i in range(BLOCKS):
        part = moved[i * block_rows : (i + 1) * block_rows].astype(jnp.float32)
        met = paired_ortho[i] if i == 0 else after(paired_ortho[i], sent[i - 1])
        sent.append(
            (part - step_scale * (ortho[i].astype(jnp.float32) + met.astype(jnp.float32))).astype(jnp.bfloat16)
        )
    back = [lax.ppermute(x, both, returned) for x in sent]
    halves = jnp.where(is_swapped, moved, jnp.concatenate(sent, axis=0)).astype(jnp.float32)
    ready = 0.5 * jnp.where(is_swapped, halves, halves + borrowed.astype(jnp.float32))
    return pl.pallas_call(
        functools.partial(last_kernel, BLOCKS),
        in_specs=[VMEM] * (1 + BLOCKS),
        out_specs=ANY,
        out_shape=jax.ShapeDtypeStruct((1, 1, fan_rows, features), jnp.bfloat16),
        scratch_shapes=[pltpu.VMEM((fan_rows, features), jnp.bfloat16), pltpu.SemaphoreType.DMA((BLOCKS,))],
        compiler_params=pltpu.CompilerParams(vmem_limit_bytes=VMEM_LIMIT),
        cost_estimate=pl.CostEstimate(flops=0, bytes_accessed=8 * fan_rows * features, transcendentals=0),
    )(ready.astype(jnp.bfloat16), *back)


def from_behind(block, axis, distance):
    devices = range(lax.axis_size(axis))
    route = [((i - distance) % len(devices), i) for i in devices]
    return lax.ppermute(block, axis, route)


def orthogonalize(tracked):
    frobenius = jnp.sqrt(jnp.sum(tracked * tracked))
    return newton_schulz((tracked / (frobenius + 1e-07)).astype(jnp.bfloat16))


def place_rows(gradient, routing, experts, slot_count):
    owned = (routing[:, None] == jnp.arange(experts, dtype=jnp.int32)[None, :]).astype(jnp.int32)
    earlier = jnp.cumsum(owned, axis=0) - owned
    position = jnp.sum(earlier * owned, axis=1)
    target = routing * slot_count + position
    selector = (
        target[None, :] == jnp.arange(experts * slot_count, dtype=jnp.int32)[:, None]
    ).astype(jnp.bfloat16)
    placed = dot(selector, gradient, ((1,), (0,))).astype(jnp.bfloat16)
    return placed.reshape(experts, slot_count, gradient.shape[1])


def general(out_grads, routes, hiddens, weights, tracker_offset, partner_bits):
    experts = lax.axis_size("expert")
    stashed = hiddens[:, 0, 0]
    steps, slot_rows = stashed.shape[:2]
    slot_count = slot_rows // experts
    direction = partner_bits[0]
    weight, offset = weights[0, 0], tracker_offset[0, 0]
    placed = [place_rows(out_grads[k, 0], routes[k, 0, :, 0], experts, slot_count) for k in range(steps)]
    arrived = lax.all_to_all(jnp.stack(placed), "expert", split_axis=1, concat_axis=1, tiled=True)
    updates = jnp.zeros(weight.shape, jnp.float32)
    for k in range(steps):
        product = dot(stashed[k], arrived[k].reshape(slot_rows, -1), ((0,), (0,)))
        gradient = (product * (1.0 / math.sqrt(slot_rows))).astype(jnp.bfloat16).astype(jnp.float32)
        summed = offset.astype(jnp.float32) + gradient
        sent = summed.astype(jnp.bfloat16)
        distance = 2**k
        partner = jnp.where(
            direction[k] == 1,
            from_behind(sent, "site", -distance),
            from_behind(sent, "site", distance),
        )
        tracked = 0.5 * (summed + partner.astype(jnp.float32))
        offset = (tracked - gradient).astype(jnp.bfloat16)
        updates = updates + orthogonalize(tracked).astype(jnp.float32)
    updated = weight.astype(jnp.float32) - step_scale * updates
    sent = updated.astype(jnp.bfloat16)
    beside = from_behind(sent, "site", -weight_hop).astype(jnp.float32) + from_behind(
        sent, "site", weight_hop
    ).astype(jnp.float32)
    return (0.5 * updated + 0.25 * beside).astype(jnp.bfloat16)[None, None]


def solution(mesh):
    in_specs = (
        P(None, "site", "expert", None),
        P(None, "site", "expert", None),
        P(None, "site", "expert", None, None),
        P("site", "expert", None, None),
        P("site", "expert", None, None),
        P("site", None),
    )
    out_specs = P("site", "expert", None, None)
    sites, experts = mesh.shape["site"], mesh.shape["expert"]
    pairs = sites == 2 * weight_hop and experts in (2, 4)
    local = paired if pairs else general
    return jax.shard_map(local, mesh=mesh, in_specs=in_specs, out_specs=out_specs, check_vma=False)
```

```python
import functools
import math

import jax
import jax.numpy as jnp
from jax import lax
from jax.experimental import pallas as pl
from jax.experimental.pallas import tpu as pltpu
from jax.sharding import PartitionSpec as P

NS_ITERS = 2
CHUNKS = 2
BLOCKS = 2
DIRECT = 1
X_LATE = True
NS_LATE = False
B_LATE = False
VMEM_LIMIT = 32 * 1024 * 1024

coef_a = 3.4445
coef_b = -4.775
coef_c = 2.0315
step_scale = 32.0
weight_hop = 4

ANY = pl.BlockSpec(memory_space=pl.ANY)
VMEM = pl.BlockSpec(memory_space=pltpu.VMEM)


def dot(a, b, dims):
    return lax.dot_general(a, b, (dims, ((), ())), preferred_element_type=jnp.float32)


def newton_schulz(*currents):
    for repeat in range(NS_ITERS):
        grams = [dot(c, c, ((1,), (1,))).astype(jnp.bfloat16) for c in currents]
        squares = [dot(g, g, ((1,), (0,))) for g in grams]
        polys = [
            (coef_b * g.astype(jnp.float32) + coef_c * q).astype(jnp.bfloat16) for g, q in zip(grams, squares)
        ]
        products = [dot(p, c, ((1,), (0,))) for p, c in zip(polys, currents)]
        currents = [(coef_a * c.astype(jnp.float32) + p).astype(jnp.bfloat16) for c, p in zip(currents, products)]
    return currents


def normalized(tracked):
    total = sum(jnp.sum(part * part) for part in tracked)
    scale = 1.0 / (jnp.sqrt(total) + 1e-07)
    return jnp.concatenate([(part * scale).astype(jnp.bfloat16) for part in tracked], axis=0)


def first_step_kernel(chunks, *refs):
    offset, grads, partners = refs[0], refs[1 : 1 + chunks], refs[1 + chunks : 1 + 2 * chunks]
    weight, blocks = refs[1 + 2 * chunks], refs[2 + 2 * chunks :]
    start, tracked = 0, []
    for k in range(chunks):
        part = slice(start, start + grads[k].shape[0])
        start = part.stop
        own = offset[part, :].astype(jnp.float32) + grads[k][...].astype(jnp.float32)
        tracked.append(0.5 * (own + partners[k][...].astype(jnp.float32)))
    (ortho,) = newton_schulz(normalized(tracked))
    rows = blocks[0].shape[0]
    for k, block in enumerate(blocks):
        part = slice(k * rows, (k + 1) * rows)
        value = weight[part, :].astype(jnp.float32) - step_scale * ortho[part, :].astype(jnp.float32)
        block[...] = value.astype(block.dtype)


def second_step_kernel(chunks, bits_first, bits_second, *refs):
    groups = [refs[i * chunks : (i + 1) * chunks] for i in range(4)]
    here0, here1, there0, there1 = groups
    blocks = refs[4 * chunks :]
    core = lax.axis_index("expert") % 2
    starts = []
    for own, use_here in (
        (here1, bits_first[0:1, 1:2] == 1 - core),
        (there0, bits_second[0:1, 1:2] == core),
    ):
        tracked = []
        for k in range(chunks):
            partner = jnp.where(use_here, here0[k][...].astype(jnp.float32), there1[k][...].astype(jnp.float32))
            tracked.append(0.5 * (own[k][...].astype(jnp.float32) + partner))
        starts.append(normalized(tracked))
    first, second = newton_schulz(*starts)
    total = -0.5 * step_scale * (first.astype(jnp.float32) + second.astype(jnp.float32))
    rows = blocks[0].shape[0]
    for k, block in enumerate(blocks):
        block[...] = total[k * rows : (k + 1) * rows, :]


def last_kernel(blocks, *refs):
    first, second, out, buffer, semaphores = refs[:blocks], refs[blocks : 2 * blocks], *refs[2 * blocks :]
    rows = first[0].shape[0]
    copies = []
    for k in range(blocks):
        part = pl.ds(k * rows, rows)
        buffer[part, :] = first[k][...] + second[k][...]
        copies.append(pltpu.make_async_copy(buffer.at[part], out.at[0, 0, part], semaphores.at[k]))
        copies[-1].start()
    for copy in copies:
        copy.wait()


def gradient_kernel(sources, with_sum, *refs):
    tokens, hidden, refs = refs[:sources], refs[sources], refs[sources + 1 :]
    rows = hidden.shape[0]
    slots = rows // sources
    count = tokens[0].shape[0] - 16
    mine = lax.axis_index("expert")
    earlier = (
        lax.broadcasted_iota(jnp.int32, (count, count), 0)
        < lax.broadcasted_iota(jnp.int32, (count, count), 1)
    ).astype(jnp.bfloat16)
    slot = lax.broadcasted_iota(jnp.int32, (slots, count), 0).astype(jnp.float32)
    taken = []
    for j in range(sources):
        named = tokens[j][count : count + 16, :count].astype(jnp.float32)
        match = jnp.where(named == mine.astype(jnp.float32), 1.0, 0.0)
        position = dot(match.astype(jnp.bfloat16), earlier, ((1,), (0,)))[0:1, :]
        chosen = jnp.where((slot == position) & (match[0:1, :] > 0.5), 1.0, 0.0).astype(jnp.bfloat16)
        start = pl.multiple_of((mine ^ j) * slots, slots)
        taken.append(dot(chosen, hidden[pl.ds(start, slots), :], ((0,), (0,))).astype(jnp.bfloat16))
    spread = jnp.concatenate(taken, axis=0)
    everything = jnp.concatenate([t[:count, :] for t in tokens], axis=0)
    product = dot(spread, everything, ((0,), (0,)))
    grad = (product * (1.0 / math.sqrt(rows))).astype(jnp.bfloat16)
    if with_sum:
        offset, refs = refs[0], refs[1:]
        summed = (offset[...].astype(jnp.float32) + grad.astype(jnp.float32)).astype(jnp.bfloat16)
        refs, sums = refs[: len(refs) // 2], refs[len(refs) // 2 :]
    start = 0
    for k, out in enumerate(refs):
        part = slice(start, start + out.shape[0])
        start = part.stop
        out[...] = grad[part, :]
        if with_sum:
            sums[k][...] = summed[part, :]


def call(kernel, operands, out_shapes, flops):
    arrays = [a[0] if isinstance(a, tuple) else a for a in operands]
    fetched = {i: a[1] for i, a in enumerate(operands) if isinstance(a, tuple)}
    shapes = [a.shape if fetched.get(i) is None else a.shape[1:] for i, a in enumerate(arrays)]
    count, results, copied = len(arrays), len(out_shapes), list(fetched)

    def body(*refs):
        sources, targets = list(refs[:count]), refs[count : count + results]
        copies = []
        for n, i in enumerate(copied):
            source = sources[i] if fetched[i] is None else sources[i].at[fetched[i]]
            buffer = refs[count + results + n]
            copies.append(pltpu.make_async_copy(source, buffer, refs[-1].at[n]))
            sources[i] = buffer
        for copy in copies:
            copy.start()
        for copy in copies:
            copy.wait()
        kernel(*sources, *targets)

    moved = sum(math.prod(s) * a.dtype.itemsize for s, a in zip(shapes, arrays))
    moved += sum(math.prod(s.shape) * s.dtype.itemsize for s in out_shapes)
    return pl.pallas_call(
        body,
        in_specs=[ANY if i in fetched else VMEM for i in range(count)],
        out_specs=[VMEM] * results,
        out_shape=out_shapes,
        scratch_shapes=[pltpu.VMEM(shapes[i], arrays[i].dtype) for i in copied]
        + [pltpu.SemaphoreType.DMA((max(1, len(copied)),))],
        compiler_params=pltpu.CompilerParams(vmem_limit_bytes=VMEM_LIMIT),
        cost_estimate=pl.CostEstimate(flops=flops, bytes_accessed=moved, transcendentals=0),
    )(*arrays)


def after(value, earlier):
    return lax.optimization_barrier((value, earlier))[0]


def paired(out_grads, routes, hiddens, weights, tracker_offset, partner_bits):
    sites, experts = lax.axis_size("site"), lax.axis_size("expert")
    half = sites // 2
    site, expert = lax.axis_index("site"), lax.axis_index("expert")
    both = ("site", "expert")

    def at(site, expert):
        return site * experts + expert

    middle, outer, matched = [], [], []
    for s in range(sites // 4):
        near, far, last_site = s + half // 2, s + half, s + half + half // 2
        for e in range(0, experts, 2):
            for worker, owner in ((near, e), (far, e + 1)):
                even, odd = at(worker, e), at(worker, e + 1)
                middle += [(at(near, owner), even), (at(far, owner), odd)]
                outer += [(at(s, owner), even), (at(last_site, owner), odd)]
                matched += [(at(far, owner), even), (at(near, owner), odd)]
    to_outer = [(b, a) for a, b in outer]
    to_matched = [(b, a) for a, b in matched]
    mates = [(e, e ^ 1) for e in range(experts)]
    beside = [(s, s ^ 1) for s in range(sites)]
    helpers = [(s, (s + 2) % sites if s % 2 else (s - 2) % sites) for s in range(sites)]
    weight, offset = weights[0, 0], tracker_offset[0, 0]
    stashed = hiddens[:, 0, 0]
    tokens, routing = out_grads[:, 0], routes[:, 0, :, 0]
    steps = tokens.shape[0]
    fan_rows, features = weight.shape
    bits = partner_bits[0]

    beside_bits = lax.ppermute(bits, "site", beside)
    send_own = beside_bits.reshape(1, -1)[:, 0:1] == site % 2
    first_bits = lax.ppermute(bits, both, outer).reshape(1, -1)
    second_bits = lax.ppermute(bits, both, matched).reshape(1, -1)

    count = tokens.shape[1]
    named = routing.astype(jnp.bfloat16).reshape(steps, 1, count)
    named = jnp.pad(named, ((0, 0), (0, 15), (0, features - count)))
    gathered = [{0: jnp.concatenate([tokens[k], named[k]], axis=0)} for k in range(steps)]
    top = experts // 2
    for k in range(steps):
        level = top
        if k > 0:
            gathered[k][0] = after(gathered[k][0], gathered[k - 1][top])
        while level >= 1:
            hop = [(e, e ^ level) for e in range(experts)]
            gathered[k].update({j ^ level: lax.ppermute(t, "expert", hop) for j, t in gathered[k].items()})
            if k == 0 and level == top:
                gathered[k][top], (send_own, first_bits, second_bits) = lax.optimization_barrier(
                    (gathered[k][top], (send_own, first_bits, second_bits))
                )
            level //= 2

    edges = [fan_rows // 16 * i // CHUNKS * 16 for i in range(CHUNKS)] + [fan_rows]
    parts = [slice(low, high) for low, high in zip(edges, edges[1:])]
    chunk = [jax.ShapeDtypeStruct((p.stop - p.start, features), jnp.bfloat16) for p in parts]
    whole = [jax.ShapeDtypeStruct((fan_rows, features), jnp.bfloat16)]
    cost = 2 * fan_rows * features * experts * count
    operands = [gathered[0][j] for j in range(experts)] + [(stashed, 0), (offset, None)]
    made = call(functools.partial(gradient_kernel, experts, True), operands, chunk * 2, cost)
    first, own = made[:CHUNKS], list(made[CHUNKS:])
    ahead = [from_behind(o, "site", -1) for o in own[:DIRECT]]
    behind = [from_behind(o, "site", 1) for o in own[:DIRECT]]
    fetched = [lax.ppermute(o, "site", helpers) for o in own[DIRECT:]]
    operands = [gathered[1][j] for j in range(experts)] + [(stashed, 1)]
    last = call(functools.partial(gradient_kernel, experts, False), operands, chunk, cost)

    use_ahead = bits.reshape(1, -1)[:, 0:1] == 1
    partners, second, here0, here1 = [], [], [], []
    for i in range(CHUNKS):
        if i < DIRECT:
            partners.append(jnp.where(use_ahead, ahead[i], after(behind[i], last[0])))
        else:
            arrived = after(fetched[i - DIRECT], last[0])
            if i == DIRECT and i > 0 and X_LATE:
                arrived = after(arrived, partners[-1])
            partners.append(lax.ppermute(jnp.where(send_own, own[i], arrived), "site", beside))
        partner = partners[i] if i == 0 else after(partners[i], second[i - 1])
        grad = first[i].astype(jnp.float32)
        tracked = 0.5 * ((offset[parts[i]].astype(jnp.float32) + grad) + partner.astype(jnp.float32))
        later = (tracked - grad).astype(jnp.bfloat16).astype(jnp.float32)
        second.append((later + last[i].astype(jnp.float32)).astype(jnp.bfloat16))
        here0.append(lax.ppermute(second[i], both, middle))
        here1.append(lax.ppermute(second[i], both, outer))

    cost = NS_ITERS * 2 * (2 * fan_rows * fan_rows * features + fan_rows**3)
    held = after(partners[-1], (second[-1], here0[0]) if NS_LATE else second[-1])
    rows = fan_rows // BLOCKS
    moved = call(
        functools.partial(first_step_kernel, CHUNKS),
        [(offset, None), *first, *partners[:-1], held, (weight, None)],
        [jax.ShapeDtypeStruct((rows, features), jnp.bfloat16)] * BLOCKS,
        cost,
    )
    here0[-1] = after(here0[-1], moved)
    there0 = [lax.ppermute(h, "expert", mates) for h in here0]
    there1 = [lax.ppermute(h, "expert", mates) for h in here1]
    lent = [after(m, (here0[-1], here1[-1]) if B_LATE else second[-1]) for m in moved]
    pairs = [(lax.ppermute(v, both, outer), lax.ppermute(v, both, matched)) for v in lent]

    update = call(
        functools.partial(second_step_kernel, CHUNKS),
        [first_bits, second_bits, *here0, *here1, *there0, *there1],
        [jax.ShapeDtypeStruct((rows, features), jnp.float32)] * BLOCKS,
        2 * cost,
    )
    results = []
    for i in range(BLOCKS):
        pair = pairs[i] if i == 0 else after(pairs[i], results[-1])
        pair = pair[0].astype(jnp.float32) + pair[1].astype(jnp.float32)
        results.append((0.5 * pair + update[i]).astype(jnp.bfloat16))
    arrived = [lax.ppermute(r, both, to_outer) for r in results] + [lax.ppermute(r, both, to_matched) for r in results]
    return pl.pallas_call(
        functools.partial(last_kernel, BLOCKS),
        in_specs=[VMEM] * (2 * BLOCKS),
        out_specs=ANY,
        out_shape=jax.ShapeDtypeStruct((1, 1, fan_rows, features), jnp.bfloat16),
        scratch_shapes=[pltpu.VMEM((fan_rows, features), jnp.bfloat16), pltpu.SemaphoreType.DMA((BLOCKS,))],
        compiler_params=pltpu.CompilerParams(vmem_limit_bytes=VMEM_LIMIT),
        cost_estimate=pl.CostEstimate(flops=0, bytes_accessed=8 * fan_rows * features, transcendentals=0),
    )(*arrived)


def from_behind(block, axis, distance):
    devices = range(lax.axis_size(axis))
    route = [((i - distance) % len(devices), i) for i in devices]
    return lax.ppermute(block, axis, route)


def orthogonalize(tracked):
    frobenius = jnp.sqrt(jnp.sum(tracked * tracked))
    return newton_schulz((tracked / (frobenius + 1e-07)).astype(jnp.bfloat16))[0]


def place_rows(gradient, routing, experts, slot_count):
    owned = (routing[:, None] == jnp.arange(experts, dtype=jnp.int32)[None, :]).astype(jnp.int32)
    earlier = jnp.cumsum(owned, axis=0) - owned
    position = jnp.sum(earlier * owned, axis=1)
    target = routing * slot_count + position
    selector = (
        target[None, :] == jnp.arange(experts * slot_count, dtype=jnp.int32)[:, None]
    ).astype(jnp.bfloat16)
    placed = dot(selector, gradient, ((1,), (0,))).astype(jnp.bfloat16)
    return placed.reshape(experts, slot_count, gradient.shape[1])


def general(out_grads, routes, hiddens, weights, tracker_offset, partner_bits):
    experts = lax.axis_size("expert")
    stashed = hiddens[:, 0, 0]
    steps, slot_rows = stashed.shape[:2]
    slot_count = slot_rows // experts
    direction = partner_bits[0]
    weight, offset = weights[0, 0], tracker_offset[0, 0]
    placed = [place_rows(out_grads[k, 0], routes[k, 0, :, 0], experts, slot_count) for k in range(steps)]
    arrived = lax.all_to_all(jnp.stack(placed), "expert", split_axis=1, concat_axis=1, tiled=True)
    updates = jnp.zeros(weight.shape, jnp.float32)
    for k in range(steps):
        product = dot(stashed[k], arrived[k].reshape(slot_rows, -1), ((0,), (0,)))
        gradient = (product * (1.0 / math.sqrt(slot_rows))).astype(jnp.bfloat16).astype(jnp.float32)
        summed = offset.astype(jnp.float32) + gradient
        sent = summed.astype(jnp.bfloat16)
        distance = 2**k
        partner = jnp.where(
            direction[k] == 1,
            from_behind(sent, "site", -distance),
            from_behind(sent, "site", distance),
        )
        tracked = 0.5 * (summed + partner.astype(jnp.float32))
        offset = (tracked - gradient).astype(jnp.bfloat16)
        updates = updates + orthogonalize(tracked).astype(jnp.float32)
    updated = weight.astype(jnp.float32) - step_scale * updates
    sent = updated.astype(jnp.bfloat16)
    beside = from_behind(sent, "site", -weight_hop).astype(jnp.float32) + from_behind(
        sent, "site", weight_hop
    ).astype(jnp.float32)
    return (0.5 * updated + 0.25 * beside).astype(jnp.bfloat16)[None, None]


def solution(mesh):
    in_specs = (
        P(None, "site", "expert", None),
        P(None, "site", "expert", None),
        P(None, "site", "expert", None, None),
        P("site", "expert", None, None),
        P("site", "expert", None, None),
        P("site", None),
    )
    out_specs = P("site", "expert", None, None)
    sites, experts = mesh.shape["site"], mesh.shape["expert"]
    pairs = sites == 2 * weight_hop and experts in (2, 4)
    local = paired if pairs else general
    return jax.shard_map(local, mesh=mesh, in_specs=in_specs, out_specs=out_specs, check_vma=False)
```

```python
import functools
import math

import jax
import jax.numpy as jnp
from jax import lax
from jax.experimental import pallas as pl
from jax.experimental.pallas import tpu as pltpu
from jax.sharding import PartitionSpec as P

NS_ITERS = 2
CHUNKS = 2
BLOCKS = 2
DIRECT = 1
VMEM_LIMIT = 32 * 1024 * 1024

coef_a = 3.4445
coef_b = -4.775
coef_c = 2.0315
step_scale = 32.0
weight_hop = 4

ANY = pl.BlockSpec(memory_space=pl.ANY)
VMEM = pl.BlockSpec(memory_space=pltpu.VMEM)


def dot(a, b, dims):
    return lax.dot_general(a, b, (dims, ((), ())), preferred_element_type=jnp.float32)


def newton_schulz(*currents):
    for repeat in range(NS_ITERS):
        grams = [dot(c, c, ((1,), (1,))).astype(jnp.bfloat16) for c in currents]
        squares = [dot(g, g, ((1,), (0,))) for g in grams]
        polys = [
            (coef_b * g.astype(jnp.float32) + coef_c * q).astype(jnp.bfloat16) for g, q in zip(grams, squares)
        ]
        products = [dot(p, c, ((1,), (0,))) for p, c in zip(polys, currents)]
        currents = [(coef_a * c.astype(jnp.float32) + p).astype(jnp.bfloat16) for c, p in zip(currents, products)]
    return currents


def normalized(tracked):
    total = sum(jnp.sum(part * part) for part in tracked)
    scale = 1.0 / (jnp.sqrt(total) + 1e-07)
    return jnp.concatenate([(part * scale).astype(jnp.bfloat16) for part in tracked], axis=0)


def row_parts(blocks):
    ends = [sum(b.shape[0] for b in blocks[: k + 1]) for k in range(len(blocks))]
    return [slice(end - b.shape[0], end) for b, end in zip(blocks, ends)]


def first_step_kernel(chunks, *refs):
    offset, grads, partners = refs[0], refs[1 : 1 + chunks], refs[1 + chunks : 1 + 2 * chunks]
    weight, blocks = refs[1 + 2 * chunks], refs[2 + 2 * chunks :]
    start, tracked = 0, []
    for k in range(chunks):
        part = slice(start, start + grads[k].shape[0])
        start = part.stop
        own = offset[part, :].astype(jnp.float32) + grads[k][...].astype(jnp.float32)
        tracked.append(0.5 * (own + partners[k][...].astype(jnp.float32)))
    (ortho,) = newton_schulz(normalized(tracked))
    for part, block in zip(row_parts(blocks), blocks):
        value = weight[part, :].astype(jnp.float32) - step_scale * ortho[part, :].astype(jnp.float32)
        block[...] = value.astype(block.dtype)


def second_step_kernel(chunks, bits_first, bits_second, *refs):
    groups = [refs[i * chunks : (i + 1) * chunks] for i in range(4)]
    here0, here1, there0, there1 = groups
    blocks = refs[4 * chunks :]
    core = lax.axis_index("expert") % 2
    starts = []
    for own, use_here in (
        (here1, bits_first[0:1, 1:2] == 1 - core),
        (there0, bits_second[0:1, 1:2] == core),
    ):
        tracked = []
        for k in range(chunks):
            partner = jnp.where(use_here, here0[k][...].astype(jnp.float32), there1[k][...].astype(jnp.float32))
            tracked.append(0.5 * (own[k][...].astype(jnp.float32) + partner))
        starts.append(normalized(tracked))
    first, second = newton_schulz(*starts)
    total = -0.5 * step_scale * (first.astype(jnp.float32) + second.astype(jnp.float32))
    for part, block in zip(row_parts(blocks), blocks):
        block[...] = total[part, :]


def last_kernel(blocks, *refs):
    first, second, out, buffer, semaphores = refs[:blocks], refs[blocks : 2 * blocks], *refs[2 * blocks :]
    copies = []
    for k, part in enumerate(row_parts(first)):
        buffer[part, :] = first[k][...] + second[k][...]
        copies.append(pltpu.make_async_copy(buffer.at[part], out.at[0, 0, part], semaphores.at[k]))
        copies[-1].start()
    for copy in copies:
        copy.wait()


def gradient_kernel(sources, with_sum, *refs):
    tokens, hidden, refs = refs[:sources], refs[sources], refs[sources + 1 :]
    rows = hidden.shape[0]
    slots = rows // sources
    count = tokens[0].shape[0] - 16
    mine = lax.axis_index("expert")
    earlier = (
        lax.broadcasted_iota(jnp.int32, (count, count), 0)
        < lax.broadcasted_iota(jnp.int32, (count, count), 1)
    ).astype(jnp.bfloat16)
    slot = lax.broadcasted_iota(jnp.int32, (slots, count), 0).astype(jnp.float32)
    taken = []
    for j in range(sources):
        named = tokens[j][count : count + 16, :count].astype(jnp.float32)
        match = jnp.where(named == mine.astype(jnp.float32), 1.0, 0.0)
        position = dot(match.astype(jnp.bfloat16), earlier, ((1,), (0,)))[0:1, :]
        chosen = jnp.where((slot == position) & (match[0:1, :] > 0.5), 1.0, 0.0).astype(jnp.bfloat16)
        start = pl.multiple_of((mine ^ j) * slots, slots)
        taken.append(dot(chosen, hidden[pl.ds(start, slots), :], ((0,), (0,))).astype(jnp.bfloat16))
    spread = jnp.concatenate(taken, axis=0)
    everything = jnp.concatenate([t[:count, :] for t in tokens], axis=0)
    product = dot(spread, everything, ((0,), (0,)))
    grad = (product * (1.0 / math.sqrt(rows))).astype(jnp.bfloat16)
    if with_sum:
        offset, refs = refs[0], refs[1:]
        summed = (offset[...].astype(jnp.float32) + grad.astype(jnp.float32)).astype(jnp.bfloat16)
        refs, sums = refs[: len(refs) // 2], refs[len(refs) // 2 :]
    start = 0
    for k, out in enumerate(refs):
        part = slice(start, start + out.shape[0])
        start = part.stop
        out[...] = grad[part, :]
        if with_sum:
            sums[k][...] = summed[part, :]


def call(kernel, operands, out_shapes, flops):
    arrays = [a[0] if isinstance(a, tuple) else a for a in operands]
    picks = [a[1] if isinstance(a, tuple) else None for a in operands]
    count = len(arrays)

    def body(*refs):
        sources = [r if p is None else r.at[p] for r, p in zip(refs[:count], picks)]
        kernel(*sources, *refs[count:])

    moved = sum(math.prod(a.shape) * a.dtype.itemsize for a in [*arrays, *out_shapes])
    return pl.pallas_call(
        body,
        in_specs=[VMEM] * count,
        out_specs=[VMEM] * len(out_shapes),
        out_shape=out_shapes,
        compiler_params=pltpu.CompilerParams(vmem_limit_bytes=VMEM_LIMIT),
        cost_estimate=pl.CostEstimate(flops=flops, bytes_accessed=moved, transcendentals=0),
    )(*arrays)


def after(value, earlier):
    return lax.optimization_barrier((value, earlier))[0]


def paired(out_grads, routes, hiddens, weights, tracker_offset, partner_bits):
    sites, experts = lax.axis_size("site"), lax.axis_size("expert")
    half = sites // 2
    site, expert = lax.axis_index("site"), lax.axis_index("expert")
    both = ("site", "expert")

    def at(site, expert):
        return site * experts + expert

    middle, outer, matched = [], [], []
    for s in range(sites // 4):
        near, far, last_site = s + half // 2, s + half, s + half + half // 2
        for e in range(0, experts, 2):
            for worker, owner in ((near, e), (far, e + 1)):
                even, odd = at(worker, e), at(worker, e + 1)
                middle += [(at(near, owner), even), (at(far, owner), odd)]
                outer += [(at(s, owner), even), (at(last_site, owner), odd)]
                matched += [(at(far, owner), even), (at(near, owner), odd)]
    to_outer = [(b, a) for a, b in outer]
    to_matched = [(b, a) for a, b in matched]
    mates = [(e, e ^ 1) for e in range(experts)]
    beside = [(s, s ^ 1) for s in range(sites)]
    helpers = [(s, (s + 2) % sites if s % 2 else (s - 2) % sites) for s in range(sites)]
    weight, offset = weights[0, 0], tracker_offset[0, 0]
    stashed = hiddens[:, 0, 0]
    tokens, routing = out_grads[:, 0], routes[:, 0, :, 0]
    steps = tokens.shape[0]
    fan_rows, features = weight.shape
    bits = partner_bits[0]

    beside_bits = lax.ppermute(bits, "site", beside)
    send_own = beside_bits.reshape(1, -1)[:, 0:1] == site % 2
    first_bits = lax.ppermute(bits, both, outer).reshape(1, -1)
    second_bits = lax.ppermute(bits, both, matched).reshape(1, -1)

    count = tokens.shape[1]
    named = routing.astype(jnp.bfloat16).reshape(steps, 1, count)
    named = jnp.pad(named, ((0, 0), (0, 15), (0, features - count)))
    gathered = [{0: jnp.concatenate([tokens[k], named[k]], axis=0)} for k in range(steps)]
    top = experts // 2

    def spread(kept, level):
        hop = [(e, e ^ level) for e in range(experts)]
        kept.update({j ^ level: lax.ppermute(t, "expert", hop) for j, t in kept.items()})

    spread(gathered[0], top)
    gathered[0][top], (send_own, first_bits, second_bits) = lax.optimization_barrier(
        (gathered[0][top], (send_own, first_bits, second_bits))
    )
    gathered[1][0] = after(gathered[1][0], gathered[0][top])
    spread(gathered[1], top)
    if top > 1:
        spread(gathered[0], 1)

    edges = [fan_rows // 16 * i // CHUNKS * 16 for i in range(CHUNKS)] + [fan_rows]
    parts = [slice(low, high) for low, high in zip(edges, edges[1:])]
    chunk = [jax.ShapeDtypeStruct((p.stop - p.start, features), jnp.bfloat16) for p in parts]
    cost = 2 * fan_rows * features * experts * count
    operands = [gathered[0][j] for j in range(experts)] + [(stashed, 0), offset]
    made = call(functools.partial(gradient_kernel, experts, True), operands, chunk * 2, cost)
    first, own = made[:CHUNKS], list(made[CHUNKS:])
    ahead = [from_behind(o, "site", -1) for o in own[:DIRECT]]
    behind = [from_behind(o, "site", 1) for o in own[:DIRECT]]
    fetched = [lax.ppermute(o, "site", helpers) for o in own[DIRECT:]]
    if top > 1:
        gathered[1][top] = after(gathered[1][top], made[0])
        spread(gathered[1], 1)
    operands = [gathered[1][j] for j in range(experts)] + [(stashed, 1)]
    last = call(functools.partial(gradient_kernel, experts, False), operands, chunk, cost)

    use_ahead = bits.reshape(1, -1)[:, 0:1] == 1
    partners, second, here0, here1 = [], [], [], []
    for i in range(CHUNKS):
        if i < DIRECT:
            partners.append(jnp.where(use_ahead, ahead[i], after(behind[i], last[0])))
        else:
            arrived = after(fetched[i - DIRECT], last[0])
            if i == DIRECT and i > 0:
                arrived = after(arrived, partners[-1])
            partners.append(lax.ppermute(jnp.where(send_own, own[i], arrived), "site", beside))
        partner = partners[i] if i == 0 else after(partners[i], second[i - 1])
        grad = first[i].astype(jnp.float32)
        tracked = 0.5 * ((offset[parts[i]].astype(jnp.float32) + grad) + partner.astype(jnp.float32))
        later = (tracked - grad).astype(jnp.bfloat16).astype(jnp.float32)
        second.append((later + last[i].astype(jnp.float32)).astype(jnp.bfloat16))
        here0.append(lax.ppermute(second[i], both, middle))
        here1.append(lax.ppermute(second[i], both, outer))

    cost = NS_ITERS * 2 * (2 * fan_rows * fan_rows * features + fan_rows**3)
    there0 = [lax.ppermute(h, "expert", mates) for h in here0[:-1]]
    there1 = [lax.ppermute(h, "expert", mates) for h in here1[:-1]]
    held = after(partners[-1], second[-1])
    sizes = [fan_rows // BLOCKS] * BLOCKS
    moved = call(
        functools.partial(first_step_kernel, CHUNKS),
        [offset, *first, *partners[:-1], held, weight],
        [jax.ShapeDtypeStruct((rows, features), jnp.bfloat16) for rows in sizes],
        cost,
    )
    here0[-1] = after(here0[-1], moved)
    there0.append(lax.ppermute(here0[-1], "expert", mates))
    there1.append(lax.ppermute(here1[-1], "expert", mates))
    lent = [after(m, (here0[-1], here1[-1])) for m in moved]
    pairs = [(lax.ppermute(v, both, outer), lax.ppermute(v, both, matched)) for v in lent]

    update = call(
        functools.partial(second_step_kernel, CHUNKS),
        [first_bits, second_bits, *here0, *here1, *there0, *there1],
        [jax.ShapeDtypeStruct((rows, features), jnp.float32) for rows in sizes],
        2 * cost,
    )
    results = []
    for i in range(BLOCKS):
        pair = pairs[i] if i == 0 else after(pairs[i], results[-1])
        pair = pair[0].astype(jnp.float32) + pair[1].astype(jnp.float32)
        results.append((0.5 * pair + update[i]).astype(jnp.bfloat16))
    arrived = [lax.ppermute(r, both, to_outer) for r in results] + [lax.ppermute(r, both, to_matched) for r in results]
    return pl.pallas_call(
        functools.partial(last_kernel, BLOCKS),
        in_specs=[VMEM] * (2 * BLOCKS),
        out_specs=ANY,
        out_shape=jax.ShapeDtypeStruct((1, 1, fan_rows, features), jnp.bfloat16),
        scratch_shapes=[pltpu.VMEM((fan_rows, features), jnp.bfloat16), pltpu.SemaphoreType.DMA((BLOCKS,))],
        compiler_params=pltpu.CompilerParams(vmem_limit_bytes=VMEM_LIMIT),
        cost_estimate=pl.CostEstimate(flops=0, bytes_accessed=8 * fan_rows * features, transcendentals=0),
    )(*arrived)


def from_behind(block, axis, distance):
    devices = range(lax.axis_size(axis))
    route = [((i - distance) % len(devices), i) for i in devices]
    return lax.ppermute(block, axis, route)


def orthogonalize(tracked):
    frobenius = jnp.sqrt(jnp.sum(tracked * tracked))
    return newton_schulz((tracked / (frobenius + 1e-07)).astype(jnp.bfloat16))[0]


def place_rows(gradient, routing, experts, slot_count):
    owned = (routing[:, None] == jnp.arange(experts, dtype=jnp.int32)[None, :]).astype(jnp.int32)
    earlier = jnp.cumsum(owned, axis=0) - owned
    position = jnp.sum(earlier * owned, axis=1)
    target = routing * slot_count + position
    selector = (
        target[None, :] == jnp.arange(experts * slot_count, dtype=jnp.int32)[:, None]
    ).astype(jnp.bfloat16)
    placed = dot(selector, gradient, ((1,), (0,))).astype(jnp.bfloat16)
    return placed.reshape(experts, slot_count, gradient.shape[1])


def general(out_grads, routes, hiddens, weights, tracker_offset, partner_bits):
    experts = lax.axis_size("expert")
    stashed = hiddens[:, 0, 0]
    steps, slot_rows = stashed.shape[:2]
    slot_count = slot_rows // experts
    direction = partner_bits[0]
    weight, offset = weights[0, 0], tracker_offset[0, 0]
    placed = [place_rows(out_grads[k, 0], routes[k, 0, :, 0], experts, slot_count) for k in range(steps)]
    arrived = lax.all_to_all(jnp.stack(placed), "expert", split_axis=1, concat_axis=1, tiled=True)
    updates = jnp.zeros(weight.shape, jnp.float32)
    for k in range(steps):
        product = dot(stashed[k], arrived[k].reshape(slot_rows, -1), ((0,), (0,)))
        gradient = (product * (1.0 / math.sqrt(slot_rows))).astype(jnp.bfloat16).astype(jnp.float32)
        summed = offset.astype(jnp.float32) + gradient
        sent = summed.astype(jnp.bfloat16)
        distance = 2**k
        partner = jnp.where(
            direction[k] == 1,
            from_behind(sent, "site", -distance),
            from_behind(sent, "site", distance),
        )
        tracked = 0.5 * (summed + partner.astype(jnp.float32))
        offset = (tracked - gradient).astype(jnp.bfloat16)
        updates = updates + orthogonalize(tracked).astype(jnp.float32)
    updated = weight.astype(jnp.float32) - step_scale * updates
    sent = updated.astype(jnp.bfloat16)
    beside = from_behind(sent, "site", -weight_hop).astype(jnp.float32) + from_behind(
        sent, "site", weight_hop
    ).astype(jnp.float32)
    return (0.5 * updated + 0.25 * beside).astype(jnp.bfloat16)[None, None]


def solution(mesh):
    in_specs = (
        P(None, "site", "expert", None),
        P(None, "site", "expert", None),
        P(None, "site", "expert", None, None),
        P("site", "expert", None, None),
        P("site", "expert", None, None),
        P("site", None),
    )
    out_specs = P("site", "expert", None, None)
    sites, experts = mesh.shape["site"], mesh.shape["expert"]
    pairs = sites == 2 * weight_hop and experts in (2, 4)
    local = paired if pairs else general
    return jax.shard_map(local, mesh=mesh, in_specs=in_specs, out_specs=out_specs, check_vma=False)
```

```python
import functools
import math

import jax
import jax.numpy as jnp
from jax import lax
from jax.experimental import pallas as pl
from jax.experimental.pallas import tpu as pltpu
from jax.sharding import PartitionSpec as P

NS_ITERS = 2
CHUNKS = 2
FIRST = 18
BLOCKS = 2
DIRECT = 1
VMEM_LIMIT = 32 * 1024 * 1024

coef_a = 3.4445
coef_b = -4.775
coef_c = 2.0315
step_scale = 32.0
weight_hop = 4

ANY = pl.BlockSpec(memory_space=pl.ANY)
VMEM = pl.BlockSpec(memory_space=pltpu.VMEM)


def dot(a, b, dims):
    return lax.dot_general(a, b, (dims, ((), ())), preferred_element_type=jnp.float32)


def newton_schulz(*currents):
    for repeat in range(NS_ITERS):
        grams = [dot(c, c, ((1,), (1,))).astype(jnp.bfloat16) for c in currents]
        squares = [dot(g, g, ((1,), (0,))) for g in grams]
        polys = [
            (coef_b * g.astype(jnp.float32) + coef_c * q).astype(jnp.bfloat16) for g, q in zip(grams, squares)
        ]
        products = [dot(p, c, ((1,), (0,))) for p, c in zip(polys, currents)]
        currents = [(coef_a * c.astype(jnp.float32) + p).astype(jnp.bfloat16) for c, p in zip(currents, products)]
    return currents


def normalized(tracked):
    total = sum(jnp.sum(part * part) for part in tracked)
    scale = 1.0 / (jnp.sqrt(total) + 1e-07)
    return jnp.concatenate([(part * scale).astype(jnp.bfloat16) for part in tracked], axis=0)


def row_parts(blocks):
    ends = [sum(b.shape[0] for b in blocks[: k + 1]) for k in range(len(blocks))]
    return [slice(end - b.shape[0], end) for b, end in zip(blocks, ends)]


def first_step_kernel(chunks, *refs):
    offset, grads, partners = refs[0], refs[1 : 1 + chunks], refs[1 + chunks : 1 + 2 * chunks]
    weight, blocks = refs[1 + 2 * chunks], refs[2 + 2 * chunks :]
    start, tracked = 0, []
    for k in range(chunks):
        part = slice(start, start + grads[k].shape[0])
        start = part.stop
        own = offset[part, :].astype(jnp.float32) + grads[k][...].astype(jnp.float32)
        tracked.append(0.5 * (own + partners[k][...].astype(jnp.float32)))
    (ortho,) = newton_schulz(normalized(tracked))
    for part, block in zip(row_parts(blocks), blocks):
        value = weight[part, :].astype(jnp.float32) - step_scale * ortho[part, :].astype(jnp.float32)
        block[...] = value.astype(block.dtype)


def second_step_kernel(chunks, bits_first, bits_second, *refs):
    groups = [refs[i * chunks : (i + 1) * chunks] for i in range(4)]
    here0, here1, there0, there1 = groups
    blocks = refs[4 * chunks :]
    core = lax.axis_index("expert") % 2
    starts = []
    for own, use_here in (
        (here1, bits_first[0:1, 1:2] == 1 - core),
        (there0, bits_second[0:1, 1:2] == core),
    ):
        tracked = []
        for k in range(chunks):
            partner = jnp.where(use_here, here0[k][...].astype(jnp.float32), there1[k][...].astype(jnp.float32))
            tracked.append(0.5 * (own[k][...].astype(jnp.float32) + partner))
        starts.append(normalized(tracked))
    first, second = newton_schulz(*starts)
    total = -0.5 * step_scale * (first.astype(jnp.float32) + second.astype(jnp.float32))
    for part, block in zip(row_parts(blocks), blocks):
        block[...] = total[part, :]


def last_kernel(blocks, *refs):
    first, second, out, buffer, semaphores = refs[:blocks], refs[blocks : 2 * blocks], *refs[2 * blocks :]
    copies = []
    for k, part in enumerate(row_parts(first)):
        buffer[part, :] = first[k][...] + second[k][...]
        copies.append(pltpu.make_async_copy(buffer.at[part], out.at[0, 0, part], semaphores.at[k]))
        copies[-1].start()
    for copy in copies:
        copy.wait()


def gradient_kernel(sources, with_sum, *refs):
    tokens, hidden, refs = refs[:sources], refs[sources], refs[sources + 1 :]
    rows = hidden.shape[0]
    slots = rows // sources
    count = tokens[0].shape[0] - 16
    mine = lax.axis_index("expert")
    earlier = (
        lax.broadcasted_iota(jnp.int32, (count, count), 0)
        < lax.broadcasted_iota(jnp.int32, (count, count), 1)
    ).astype(jnp.bfloat16)
    slot = lax.broadcasted_iota(jnp.int32, (slots, count), 0).astype(jnp.float32)
    taken = []
    for j in range(sources):
        named = tokens[j][count : count + 16, :count].astype(jnp.float32)
        match = jnp.where(named == mine.astype(jnp.float32), 1.0, 0.0)
        position = dot(match.astype(jnp.bfloat16), earlier, ((1,), (0,)))[0:1, :]
        chosen = jnp.where((slot == position) & (match[0:1, :] > 0.5), 1.0, 0.0).astype(jnp.bfloat16)
        start = pl.multiple_of((mine ^ j) * slots, slots)
        taken.append(dot(chosen, hidden[pl.ds(start, slots), :], ((0,), (0,))).astype(jnp.bfloat16))
    spread = jnp.concatenate(taken, axis=0)
    everything = jnp.concatenate([t[:count, :] for t in tokens], axis=0)
    product = dot(spread, everything, ((0,), (0,)))
    grad = (product * (1.0 / math.sqrt(rows))).astype(jnp.bfloat16)
    if with_sum:
        offset, refs = refs[0], refs[1:]
        summed = (offset[...].astype(jnp.float32) + grad.astype(jnp.float32)).astype(jnp.bfloat16)
        refs, sums = refs[: len(refs) // 2], refs[len(refs) // 2 :]
    start = 0
    for k, out in enumerate(refs):
        part = slice(start, start + out.shape[0])
        start = part.stop
        out[...] = grad[part, :]
        if with_sum:
            sums[k][...] = summed[part, :]


def call(kernel, operands, out_shapes, flops):
    arrays = [a[0] if isinstance(a, tuple) else a for a in operands]
    picks = [a[1] if isinstance(a, tuple) else None for a in operands]
    count = len(arrays)

    def body(*refs):
        sources = [r if p is None else r.at[p] for r, p in zip(refs[:count], picks)]
        kernel(*sources, *refs[count:])

    moved = sum(math.prod(a.shape) * a.dtype.itemsize for a in [*arrays, *out_shapes])
    return pl.pallas_call(
        body,
        in_specs=[VMEM] * count,
        out_specs=[VMEM] * len(out_shapes),
        out_shape=out_shapes,
        compiler_params=pltpu.CompilerParams(vmem_limit_bytes=VMEM_LIMIT),
        cost_estimate=pl.CostEstimate(flops=flops, bytes_accessed=moved, transcendentals=0),
    )(*arrays)


def after(value, earlier):
    return lax.optimization_barrier((value, earlier))[0]


def paired(out_grads, routes, hiddens, weights, tracker_offset, partner_bits):
    sites, experts = lax.axis_size("site"), lax.axis_size("expert")
    half = sites // 2
    site, expert = lax.axis_index("site"), lax.axis_index("expert")
    both = ("site", "expert")

    def at(site, expert):
        return site * experts + expert

    middle, outer, matched = [], [], []
    for s in range(sites // 4):
        near, far, last_site = s + half // 2, s + half, s + half + half // 2
        for e in range(0, experts, 2):
            for worker, owner in ((near, e), (far, e + 1)):
                even, odd = at(worker, e), at(worker, e + 1)
                middle += [(at(near, owner), even), (at(far, owner), odd)]
                outer += [(at(s, owner), even), (at(last_site, owner), odd)]
                matched += [(at(far, owner), even), (at(near, owner), odd)]
    to_outer = [(b, a) for a, b in outer]
    to_matched = [(b, a) for a, b in matched]
    mates = [(e, e ^ 1) for e in range(experts)]
    beside = [(s, s ^ 1) for s in range(sites)]
    helpers = [(s, (s + 2) % sites if s % 2 else (s - 2) % sites) for s in range(sites)]
    weight, offset = weights[0, 0], tracker_offset[0, 0]
    stashed = hiddens[:, 0, 0]
    tokens, routing = out_grads[:, 0], routes[:, 0, :, 0]
    steps = tokens.shape[0]
    fan_rows, features = weight.shape
    bits = partner_bits[0]

    beside_bits = lax.ppermute(bits, "site", beside)
    send_own = beside_bits.reshape(1, -1)[:, 0:1] == site % 2
    first_bits = lax.ppermute(bits, both, outer).reshape(1, -1)
    second_bits = lax.ppermute(bits, both, matched).reshape(1, -1)

    count = tokens.shape[1]
    named = routing.astype(jnp.bfloat16).reshape(steps, 1, count)
    named = jnp.pad(named, ((0, 0), (0, 15), (0, features - count)))
    gathered = [{0: jnp.concatenate([tokens[k], named[k]], axis=0)} for k in range(steps)]
    top = experts // 2

    def spread(kept, level):
        hop = [(e, e ^ level) for e in range(experts)]
        kept.update({j ^ level: lax.ppermute(t, "expert", hop) for j, t in kept.items()})

    spread(gathered[0], top)
    gathered[0][top], (send_own, first_bits, second_bits) = lax.optimization_barrier(
        (gathered[0][top], (send_own, first_bits, second_bits))
    )
    gathered[1][0] = after(gathered[1][0], gathered[0][top])
    spread(gathered[1], top)
    if top > 1:
        spread(gathered[0], 1)

    edges = [0, fan_rows // 32 * FIRST, fan_rows]
    parts = [slice(low, high) for low, high in zip(edges, edges[1:])]
    chunk = [jax.ShapeDtypeStruct((p.stop - p.start, features), jnp.bfloat16) for p in parts]
    cost = 2 * fan_rows * features * experts * count
    operands = [gathered[0][j] for j in range(experts)] + [(stashed, 0), offset]
    made = call(functools.partial(gradient_kernel, experts, True), operands, chunk * 2, cost)
    first, own = made[:CHUNKS], list(made[CHUNKS:])
    ahead = [from_behind(o, "site", -1) for o in own[:DIRECT]]
    behind = [from_behind(o, "site", 1) for o in own[:DIRECT]]
    fetched = [lax.ppermute(o, "site", helpers) for o in own[DIRECT:]]
    if top > 1:
        gathered[1][top] = after(gathered[1][top], made[0])
        spread(gathered[1], 1)
    operands = [gathered[1][j] for j in range(experts)] + [(stashed, 1)]
    last = call(functools.partial(gradient_kernel, experts, False), operands, chunk, cost)

    use_ahead = bits.reshape(1, -1)[:, 0:1] == 1
    partners, second, here0, here1 = [], [], [], []
    for i in range(CHUNKS):
        if i < DIRECT:
            partners.append(jnp.where(use_ahead, ahead[i], after(behind[i], last[0])))
        else:
            arrived = after(fetched[i - DIRECT], last[0])
            if i == DIRECT and i > 0:
                arrived = after(arrived, partners[-1])
            partners.append(lax.ppermute(jnp.where(send_own, own[i], arrived), "site", beside))
        partner = partners[i] if i == 0 else after(partners[i], second[i - 1])
        grad = first[i].astype(jnp.float32)
        tracked = 0.5 * ((offset[parts[i]].astype(jnp.float32) + grad) + partner.astype(jnp.float32))
        later = (tracked - grad).astype(jnp.bfloat16).astype(jnp.float32)
        second.append((later + last[i].astype(jnp.float32)).astype(jnp.bfloat16))
        here0.append(lax.ppermute(second[i], both, middle))
        here1.append(lax.ppermute(second[i], both, outer))

    cost = NS_ITERS * 2 * (2 * fan_rows * fan_rows * features + fan_rows**3)
    there0 = [lax.ppermute(h, "expert", mates) for h in here0[:-1]]
    there1 = [lax.ppermute(h, "expert", mates) for h in here1[:-1]]
    held = after(partners[-1], second[-1])
    sizes = [fan_rows // BLOCKS] * BLOCKS
    moved = call(
        functools.partial(first_step_kernel, CHUNKS),
        [offset, *first, *partners[:-1], held, weight],
        [jax.ShapeDtypeStruct((rows, features), jnp.bfloat16) for rows in sizes],
        cost,
    )
    here0[-1] = after(here0[-1], moved)
    there0.append(lax.ppermute(here0[-1], "expert", mates))
    there1.append(lax.ppermute(here1[-1], "expert", mates))
    lent = [after(m, (here0[-1], here1[-1])) for m in moved]
    pairs = [(lax.ppermute(v, both, outer), lax.ppermute(v, both, matched)) for v in lent]

    update = call(
        functools.partial(second_step_kernel, CHUNKS),
        [first_bits, second_bits, *here0, *here1, *there0, *there1],
        [jax.ShapeDtypeStruct((rows, features), jnp.float32) for rows in sizes],
        2 * cost,
    )
    results = []
    for i in range(BLOCKS):
        pair = pairs[i] if i == 0 else after(pairs[i], results[-1])
        pair = pair[0].astype(jnp.float32) + pair[1].astype(jnp.float32)
        results.append((0.5 * pair + update[i]).astype(jnp.bfloat16))
    arrived = [lax.ppermute(r, both, to_outer) for r in results] + [lax.ppermute(r, both, to_matched) for r in results]
    return pl.pallas_call(
        functools.partial(last_kernel, BLOCKS),
        in_specs=[VMEM] * (2 * BLOCKS),
        out_specs=ANY,
        out_shape=jax.ShapeDtypeStruct((1, 1, fan_rows, features), jnp.bfloat16),
        scratch_shapes=[pltpu.VMEM((fan_rows, features), jnp.bfloat16), pltpu.SemaphoreType.DMA((BLOCKS,))],
        compiler_params=pltpu.CompilerParams(vmem_limit_bytes=VMEM_LIMIT),
        cost_estimate=pl.CostEstimate(flops=0, bytes_accessed=8 * fan_rows * features, transcendentals=0),
    )(*arrived)


def from_behind(block, axis, distance):
    devices = range(lax.axis_size(axis))
    route = [((i - distance) % len(devices), i) for i in devices]
    return lax.ppermute(block, axis, route)


def orthogonalize(tracked):
    frobenius = jnp.sqrt(jnp.sum(tracked * tracked))
    return newton_schulz((tracked / (frobenius + 1e-07)).astype(jnp.bfloat16))[0]


def place_rows(gradient, routing, experts, slot_count):
    owned = (routing[:, None] == jnp.arange(experts, dtype=jnp.int32)[None, :]).astype(jnp.int32)
    earlier = jnp.cumsum(owned, axis=0) - owned
    position = jnp.sum(earlier * owned, axis=1)
    target = routing * slot_count + position
    selector = (
        target[None, :] == jnp.arange(experts * slot_count, dtype=jnp.int32)[:, None]
    ).astype(jnp.bfloat16)
    placed = dot(selector, gradient, ((1,), (0,))).astype(jnp.bfloat16)
    return placed.reshape(experts, slot_count, gradient.shape[1])


def general(out_grads, routes, hiddens, weights, tracker_offset, partner_bits):
    experts = lax.axis_size("expert")
    stashed = hiddens[:, 0, 0]
    steps, slot_rows = stashed.shape[:2]
    slot_count = slot_rows // experts
    direction = partner_bits[0]
    weight, offset = weights[0, 0], tracker_offset[0, 0]
    placed = [place_rows(out_grads[k, 0], routes[k, 0, :, 0], experts, slot_count) for k in range(steps)]
    arrived = lax.all_to_all(jnp.stack(placed), "expert", split_axis=1, concat_axis=1, tiled=True)
    updates = jnp.zeros(weight.shape, jnp.float32)
    for k in range(steps):
        product = dot(stashed[k], arrived[k].reshape(slot_rows, -1), ((0,), (0,)))
        gradient = (product * (1.0 / math.sqrt(slot_rows))).astype(jnp.bfloat16).astype(jnp.float32)
        summed = offset.astype(jnp.float32) + gradient
        sent = summed.astype(jnp.bfloat16)
        distance = 2**k
        partner = jnp.where(
            direction[k] == 1,
            from_behind(sent, "site", -distance),
            from_behind(sent, "site", distance),
        )
        tracked = 0.5 * (summed + partner.astype(jnp.float32))
        offset = (tracked - gradient).astype(jnp.bfloat16)
        updates = updates + orthogonalize(tracked).astype(jnp.float32)
    updated = weight.astype(jnp.float32) - step_scale * updates
    sent = updated.astype(jnp.bfloat16)
    beside = from_behind(sent, "site", -weight_hop).astype(jnp.float32) + from_behind(
        sent, "site", weight_hop
    ).astype(jnp.float32)
    return (0.5 * updated + 0.25 * beside).astype(jnp.bfloat16)[None, None]


def solution(mesh):
    in_specs = (
        P(None, "site", "expert", None),
        P(None, "site", "expert", None),
        P(None, "site", "expert", None, None),
        P("site", "expert", None, None),
        P("site", "expert", None, None),
        P("site", None),
    )
    out_specs = P("site", "expert", None, None)
    sites, experts = mesh.shape["site"], mesh.shape["expert"]
    pairs = sites == 2 * weight_hop and experts in (2, 4)
    local = paired if pairs else general
    return jax.shard_map(local, mesh=mesh, in_specs=in_specs, out_specs=out_specs, check_vma=False)
```
